256 devices in a mesh: section: 4 (over x), row: 64 (over y, z, core).
Axes of the slice: x: 4, y: 4, z: 8, core: 2. Of those that a mesh axis runs over, the one named last changes fastest.
Arguments:
- object_slices: float32 [4, 2, 1024, 1024], P('section', None, 'row'), may hold values from -5 to 5
- probe_spec: float32 [2, 1024, 1024], P(None, 'row'), may hold values from -5 to 5
- offsets: int32 [2, 2], replicated, may hold values from 0 to 1023
- measured: float32 [2, 1024, 1024], P(None, 'row'), may hold values from 0.2 to 3
Outputs:
- object_grad: float32 [4, 2, 1024, 1024], P('section', None, 'row')
The draws below stay inside these ranges and needn't reach their ends.
All inputs are finite; a program needn't handle non-finite values.
Results may differ from the reference program's by a relative error of at most 0.0003.
Values sent between devices are 32-bit elements; how exact they have to be, the bound alone decides.
No kernel may reach another device: no remote copies, remote signals or barrier semaphores. Data moves between devices by JAX's collectives and lax.ppermute only.
A program may use at most 128 MiB of HBM per device.

```python
import math
import jax
import jax.numpy as jnp

N = 1024
WAVES = 2
SLICES = 4


def plant(drawn, rng, smallest, top_value):
    spot = [jax.random.randint(jax.random.fold_in(rng, axis), (), 0, length) for axis, length in enumerate(drawn.shape)]
    longest = drawn.shape.index(max(drawn.shape))
    next_to = spot[:longest] + [(spot[longest] + 1) % drawn.shape[longest]] + spot[longest + 1:]
    return drawn.at[tuple(spot)].set(smallest).at[tuple(next_to)].set(top_value)


def level_of(rng, dims, pieces, low, top_value):
    level = 1.0
    for dim, blocks in pieces:
        draws = jax.random.uniform(jax.random.fold_in(jax.random.fold_in(rng, 6), dim), (blocks,), jnp.float32, low / len(pieces), top_value / len(pieces))
        level = level * jnp.repeat(jnp.exp(draws), dims[dim] // blocks).reshape((-1,) + (1,) * (len(dims) - 1 - dim))
    return level


def scatter_about(key, shape, scale, most, split=(), kind=jnp.bfloat16):
    values = scale * jax.random.normal(key, shape, jnp.float32)
    if split:
        values = values * level_of(key, shape, split, -0.22, 0.18)
    return jnp.clip(values, -most, most).astype(kind)


def setup_inputs(seed: int = 0) -> dict:
    keys = jax.random.split(jax.random.key(seed), 5)
    return {
        "object_slices": scatter_about(keys[0], (SLICES, 2, N, N), 0.7, 5.0, ((0, 4), (2, 64)), jnp.float32),
        "probe_spec": scatter_about(keys[1], (2, N, N), 0.7, 5.0, ((1, 64),), jnp.float32),
        "offsets": plant(jax.random.randint(keys[2], (WAVES, 2), 0, N), jax.random.fold_in(keys[2], 1), 0, N - 1).astype(jnp.int32),
        "measured": jnp.clip(jnp.exp(math.log(3.0) - 2.7080502 * jax.random.uniform(keys[3], (WAVES, N, N), jnp.float32) ** level_of(keys[3], (WAVES, N, N), ((1, 64),), -0.2, 0.2)), 0.2, 3.0),
    }


fresnel_coef = 0.37

def reorder(stored):
    lead = stored.shape[:-2]
    moved = stored.reshape(lead + (2, N // 2, N))
    moved = jnp.swapaxes(moved, -3, -2).reshape(lead + (N, N))
    moved = moved.reshape(lead + (N, 2, N // 2))
    return jnp.swapaxes(moved, -2, -1).reshape(lead + (N, N))

def reference(object_slices, probe_spec, offsets, measured):
    freq = jnp.arange(N, dtype=jnp.int32)
    signed = jnp.where(freq < N // 2, freq, freq - N)
    square = signed * signed
    phase = -math.pi * fresnel_coef / N * (square[:, None] + square[None, :]).astype(jnp.float32)
    propagator = jnp.cos(phase) + 1j * jnp.sin(phase)
    spectrum = (probe_spec[0] + 1j * probe_spec[1]).T
    targets = jnp.swapaxes(measured, 1, 2)

    def loss_of(real_part, imag_part):
        field = reorder(real_part) + 1j * reorder(imag_part)
        total = jnp.zeros((), jnp.float32)
        for wave in range(WAVES):
            turns = (freq[:, None] * offsets[wave, 0] + freq[None, :] * offsets[wave, 1]) % N
            angle = 2.0 * math.pi / N * turns.astype(jnp.float32)
            ramp = jnp.cos(angle) - 1j * jnp.sin(angle)
            wavefield = jnp.fft.ifft2(spectrum * ramp, norm='ortho')
            for layer in range(SLICES):
                outgoing = jnp.fft.fft2(field[layer] * wavefield, norm='ortho')
                if layer < SLICES - 1:
                    wavefield = jnp.fft.ifft2(propagator * outgoing, norm='ortho')
            power = jnp.real(outgoing) ** 2 + jnp.imag(outgoing) ** 2
            total = total + 0.125 * jnp.sum((power - targets[wave]) ** 2)
        return total
    grads = jax.grad(loss_of, argnums=(0, 1))(object_slices[:, 0], object_slices[:, 1])
    return jnp.stack(grads, axis=1)
```

```python
import math

import jax
import jax.numpy as jnp
import numpy as np
from jax import lax
from jax.experimental import pallas as pl
from jax.experimental.pallas import tpu as pltpu
from jax.sharding import PartitionSpec as P


N = 1024
B = 64
T = 16
L = T * T
fresnel_coef = 0.37
f32 = jnp.float32
bf16 = jnp.bfloat16


def split2(value):
    high = value.astype(bf16)
    return high, (value - high.astype(f32)).astype(bf16)


def np_split2(table):
    table = np.asarray(table, np.float64).astype(np.float32)
    high = table.astype(bf16)
    low = (table - high.astype(np.float32)).astype(bf16)
    return high, low


def left_table(cosine, sine):
    both = np.concatenate([cosine, sine], axis=0)
    high, low = np_split2(both)
    return np.concatenate([high, low, high], axis=1)


def pair(angle, scale=1.0):
    return np.stack([np.cos(angle), np.sin(angle)]).astype(np.float32) * np.float32(scale)


def complex_matrix(angle, scale):
    cosine, sine = np.cos(angle) * scale, np.sin(angle) * scale
    return np.concatenate(
        [np.concatenate([cosine, -sine], axis=1), np.concatenate([sine, cosine], axis=1)], axis=0
    )


def make_tables():
    two_pi = 2.0 * math.pi
    r32 = np.arange(32)
    r16 = np.arange(16)
    r8 = np.arange(8)
    blocks = np.arange(B)
    hb, ab = blocks // 32, blocks % 32
    lane_v, lane_t = np.repeat(r16, 16), np.tile(r16, 16)
    tab = {}
    angle = two_pi * np.outer(r32, r32) / 32
    eye2 = np.eye(2)
    tab["ly"] = left_table(np.kron(eye2, np.cos(angle)) / 8, np.kron(eye2, np.sin(angle)) / 8)
    tab["ty"] = pair(two_pi * (2 * lane_t[None, :] + hb[:, None]) * ab[:, None] / N)
    small = two_pi * np.outer(r16, r16) / 16
    mat = complex_matrix(small, 0.25)
    mat = mat.reshape(2, 16, 2, 16)
    full = np.einsum("atbk,vw->avtbwk", mat, np.eye(8)).reshape(256, 256)
    tab["ry"] = np.stack(np_split2(full))
    half = np.broadcast_to(two_pi * lane_t[None, :] / 32, (8, L))
    tab["by"] = pair(half)
    tab["by0"] = pair(np.broadcast_to(two_pi * lane_v[None, :] / 32, (8, L)))
    q = 2 * ab + hb
    angle = two_pi * np.outer(blocks, q) / B
    tab["lxf"] = left_table(np.cos(angle) / 8, np.sin(angle) / 8)
    tab["lxi"] = left_table(np.cos(angle.T) / 8, np.sin(angle.T) / 8)
    place = lane_v // 8 + 2 * (lane_v % 8)
    tab["tx"] = pair(two_pi * q[:, None] * place[None, :] / N)
    mat = complex_matrix(two_pi * np.outer(r8, r8) / 8, 0.25).reshape(2, 8, 2, 8)
    full = np.einsum("avbw,ts->avtbws", mat, np.eye(16)).reshape(256, 256)
    tab["rx"] = np.stack(np_split2(full))
    tab["bx"] = pair(np.broadcast_to(two_pi * np.repeat(r8, 16)[None, :] / 16, (8, 128)))
    signed = lambda freq: np.where(freq < N // 2, freq, freq - N).astype(np.float64)
    ky = ab[:, None] + 32 * lane_t[None, :] + 512 * hb[:, None]
    kx = 16 * blocks[:, None] + place[None, :]
    tab["hy"] = pair(-math.pi * fresnel_coef / N * signed(ky) ** 2)
    tab["hx"] = pair(-math.pi * fresnel_coef / N * signed(kx) ** 2)
    mat = complex_matrix(-small, 0.25).reshape(2, 16, 2, 16)
    order = np.zeros((16, 16))
    spot = np.arange(16)
    order[spot // 8 + 2 * (spot % 8), spot] = 1.0
    full = np.einsum("akbt,uw->akubwt", mat, order).reshape(512, 512)
    tab["ry0"] = np.stack(np_split2(full))
    tab["pm"] = np.einsum("kl,uw->kuwl", np.eye(16), order).reshape(256, 256).astype(bf16)
    return tab


TAB = make_tables()


def mul(a, t):
    return a[0] * t[0] - a[1] * t[1], a[0] * t[1] + a[1] * t[0]


def mul_conj(a, t):
    return a[0] * t[0] + a[1] * t[1], a[1] * t[0] - a[0] * t[1]


def left(table, a, sign):
    high, low = split2(jnp.concatenate(a, axis=1))
    stacked = jnp.concatenate([high, high, low], axis=0)
    out = jnp.dot(table, stacked, preferred_element_type=f32)
    c_re, c_im, s_re, s_im = out[:B, :L], out[:B, L:], out[B:, :L], out[B:, L:]
    if sign > 0:
        return c_re + s_im, c_im - s_re
    return c_re - s_im, c_im + s_re


def times(data, table):
    rows = data.shape[0]
    high, low = split2(data)
    out = jnp.dot(jnp.concatenate([high, low], axis=0), table[0], preferred_element_type=f32)
    return out[:rows] + out[rows:] + jnp.dot(high, table[1], preferred_element_type=f32)


def right(table, a, sign):
    re, im = a
    if sign < 0:
        im = -im
    stacked = jnp.concatenate(
        [
            jnp.concatenate([re[:, :128], im[:, :128]], axis=1),
            jnp.concatenate([re[:, 128:], im[:, 128:]], axis=1),
        ],
        axis=0,
    )
    out = times(stacked, table)
    re = jnp.concatenate([out[:B, :128], out[B:, :128]], axis=1)
    im = jnp.concatenate([out[:B, 128:], out[B:, 128:]], axis=1)
    return (re, im) if sign > 0 else (re, -im)


def rows_join(a, b):
    return tuple(jnp.concatenate([x, y], axis=0) for x, y in zip(a, b))


def lanes_join(a, b):
    return tuple(jnp.concatenate([x, y], axis=1) for x, y in zip(a, b))


def plus(a, b):
    return a[0] + b[0], a[1] + b[1]


def minus(a, b):
    return a[0] - b[0], a[1] - b[1]


def y_forward(a, tab):
    a = left(tab["ly"], a, 1)
    a = mul_conj(a, tab["ty"])
    a = right(tab["ry"], a, 1)
    first = tuple(x[:32] for x in a)
    second = mul_conj(tuple(x[32:] for x in a), tuple(x[:1] for x in tab["by"]))
    return rows_join(plus(first, second), minus(first, second))


def y_unfold(a, turn):
    first, second = tuple(x[:32] for x in a), tuple(x[32:] for x in a)
    return plus(first, second), mul(minus(first, second), tuple(x[:1] for x in turn))


def y_inverse(a, tab):
    a = right(tab["ry"], rows_join(*y_unfold(a, tab["by"])), -1)
    a = mul(a, tab["ty"])
    return left(tab["ly"], a, -1)


def x_forward(a, tab):
    first, second = tuple(x[:, :128] for x in a), tuple(x[:, 128:] for x in a)
    turned = mul_conj(minus(first, second), tuple(x[:1] for x in tab["bx"]))
    a = right(tab["rx"], lanes_join(plus(first, second), turned), 1)
    a = mul_conj(a, tab["tx"])
    return left(tab["lxf"], a, 1)


def x_inverse(a, tab):
    a = left(tab["lxi"], a, -1)
    a = mul(a, tab["tx"])
    a = right(tab["rx"], a, -1)
    first = tuple(x[:, :128] for x in a)
    second = mul(tuple(x[:, 128:] for x in a), tuple(x[:1] for x in tab["bx"]))
    return lanes_join(plus(first, second), minus(first, second))


def spread(block):
    turned = block.T
    halves = [
        jnp.concatenate([turned[base + 32 * v : base + 32 * v + 32] for v in range(T)], axis=1)
        for base in (0, 512)
    ]
    return jnp.concatenate(halves, axis=0)


def collect(block):
    parts = [
        block[32 * h : 32 * h + 32, T * v : T * v + T] for h in range(2) for v in range(T)
    ]
    return jnp.concatenate(parts, axis=0).T


Y_TABLES = ("ly", "ty", "ry", "by", "hy")
X_TABLES = ("lxf", "lxi", "tx", "rx", "bx", "hx")


def parts_of(value, at=0):
    return value[:, at : at + L], value[:, at + L : at + 2 * L]


def first_math(tab, obj, probe, target, dy, dx, row_pos):
    lanes = lax.broadcasted_iota(jnp.int32, (8, N), 1)
    which = lax.broadcasted_iota(jnp.int32, (8, N), 0)
    turns = (lanes * dy - 256 * which) & (N - 1)
    wave = jnp.cos(turns.astype(f32) * f32(2.0 * math.pi / N))
    cos_y, sin_y = wave[0:1], wave[1:2]
    kx = lax.broadcasted_iota(jnp.int32, (T, 128), 0) + row_pos * T
    lane = lax.broadcasted_iota(jnp.int32, (T, 128), 1)
    turns = (kx * dx - 256 * lane) & (N - 1)
    wave = jnp.cos(turns.astype(f32) * f32(2.0 * math.pi / N))
    cos_x, sin_x = wave[:, 0:1], wave[:, 1:2]
    ramp = (cos_y * cos_x - sin_y * sin_x, cos_y * sin_x + sin_y * cos_x)
    shifted = mul_conj(probe, ramp)
    spec = tuple(spread(x) for x in shifted)
    spec = rows_join(*y_unfold(spec, tab["by0"]))
    out = times(jnp.concatenate(spec, axis=1), tab["ry0"])
    field = left(tab["ly"], mul((out[:, :L], out[:, L:]), tab["ty"]), -1)
    target = spread(target)
    high, rest = split2(target)
    left_over = target - high.astype(f32)
    middle = left_over.astype(bf16)
    lowest = (left_over - middle.astype(f32)).astype(bf16)
    moved = jnp.dot(
        jnp.concatenate([high, middle, lowest], axis=0), tab["pm"], preferred_element_type=f32
    )
    target = moved[:B] + (moved[B : 2 * B] + moved[2 * B :])
    planes = tuple(spread(x) for x in obj)
    return jnp.concatenate(field + (target,) + planes, axis=1), jnp.concatenate(planes, axis=1)


def forward_of(axis):
    return y_forward if axis == "y" else x_forward


def inverse_of(axis):
    return y_inverse if axis == "y" else x_inverse


def propagate(axis, a, tab, conj):
    spec = forward_of(axis)(a, tab)
    times_h = mul_conj if conj else mul
    return inverse_of(axis)(times_h(spec, tab["h" + axis]), tab)


def pick(own, others, pos, home):
    out = own
    for step, value in enumerate(others, start=1):
        out = jnp.where((pos - home) % 4 == step, value, out)
    return out


VMEM_LIMIT = 40 * 1024 * 1024


def call(body, names, operands, out_shapes, scalars=()):
    tables = [jnp.asarray(TAB[name]) for name in names]
    smem = len(scalars)
    count = smem + len(operands)

    def kernel(*refs):
        scalar_refs = refs[:smem]
        ins = refs[smem:count]
        table_refs = refs[count : count + len(names)]
        outs = refs[count + len(names) :]
        tab = {}
        for name, ref in zip(names, table_refs):
            if name in ("ly", "lxf", "lxi", "pm"):
                tab[name] = ref[...]
            else:
                tab[name] = (ref[0], ref[1])
        body(tab, scalar_refs, ins, outs)

    return pl.pallas_call(
        kernel,
        out_shape=[jax.ShapeDtypeStruct(shape, f32) for shape in out_shapes],
        in_specs=[pl.BlockSpec(memory_space=pltpu.SMEM)] * smem
        + [pl.BlockSpec(memory_space=pltpu.VMEM)] * (len(operands) + len(names)),
        out_specs=[pl.BlockSpec(memory_space=pltpu.VMEM)] * len(out_shapes),
        compiler_params=pltpu.CompilerParams(vmem_limit_bytes=VMEM_LIMIT),
    )(*scalars, *operands, *tables)


def exchange(value):
    return lax.all_to_all(value, "row", split_axis=0, concat_axis=0, tiled=True)


def shards(object_slices, probe_spec, offsets, measured):
    def spread_slices(value, homes):
        return [
            lax.ppermute(value, "section", [(home, (home + step) % 4) for home in homes])
            for step in (1, 2, 3)
        ]

    def first(tab, scalars, ins, outs):
        wave = lax.axis_index("section") % 2
        row_pos = lax.axis_index("row")
        obj, probe, target = ins
        sent, planes = first_math(
            tab,
            (obj[0, 0], obj[0, 1]),
            (probe[0], probe[1]),
            jnp.where(wave == 0, target[0], target[1]),
            scalars[0][wave, 0],
            scalars[0][wave, 1],
            row_pos,
        )
        outs[0][...] = sent
        outs[1][...] = planes

    sent, planes = call(
        first,
        ("ly", "ty", "by0", "ry0", "pm"),
        (object_slices, probe_spec, measured),
        ((B, 5 * L), (B, 2 * L)),
        scalars=(offsets,),
    )
    row_objects = spread_slices(planes, (0, 2))
    got = exchange(sent)

    def chosen(ins, home):
        pos = lax.axis_index("section")
        return parts_of(pick(ins[0], ins[1:], pos, home))

    def second(tab, scalars, ins, outs):
        value = ins[0][...]
        psi = x_inverse(parts_of(value), tab)
        outs[0][...] = jnp.concatenate(psi, axis=1)
        obj = chosen([ref[...] for ref in ins[1:]], 0)
        a = propagate("x", mul(psi, obj), tab, False)
        outs[1][...] = jnp.concatenate(a, axis=1)
        outs[2][...] = value[:, 3 * L :]
        outs[3][...] = value[:, 2 * L : 3 * L]

    psi0, sent, columns, target = call(
        second,
        X_TABLES,
        (got, planes, *row_objects),
        ((B, 2 * L), (B, 2 * L), (B, 2 * L), (B, L)),
    )
    column_objects = spread_slices(columns, (1, 3))
    row_all = (planes, *row_objects)
    column_all = (columns, *column_objects)

    def inner(axis, home, last):
        def body(tab, scalars, ins, outs):
            psi = propagate(axis, parts_of(ins[0][...]), tab, False)
            outs[0][...] = jnp.concatenate(psi, axis=1)
            a = mul(psi, chosen([ref[...] for ref in ins[1:]], home))
            a = y_forward(a, tab) if last else propagate(axis, a, tab, False)
            outs[1][...] = jnp.concatenate(a, axis=1)

        return body

    square = ((B, 2 * L), (B, 2 * L))
    psi1, sent = call(inner("y", 1, False), Y_TABLES, (exchange(sent), *column_all), square)
    psi2, sent = call(inner("x", 2, False), X_TABLES, (exchange(sent), *row_all), square)
    psi3, sent = call(inner("y", 3, True), Y_TABLES, (exchange(sent), *column_all), square)

    def far(tab, scalars, ins, outs):
        phi = x_forward(parts_of(ins[0][...]), tab)
        weight = 0.5 * (phi[0] * phi[0] + phi[1] * phi[1] - ins[1][...])
        a = x_inverse((phi[0] * weight, phi[1] * weight), tab)
        outs[0][...] = jnp.concatenate(a, axis=1)

    (sent,) = call(far, X_TABLES, (exchange(sent), target), ((B, 2 * L),))

    def back(axis, home, top, both):
        def body(tab, scalars, ins, outs):
            a = parts_of(ins[0][...])
            adj = y_inverse(a, tab) if top else propagate(axis, a, tab, True)
            grad = mul_conj(adj, parts_of(ins[1][...]))
            a = mul_conj(adj, chosen([ref[...] for ref in ins[2:]], home))
            a = propagate(axis, a, tab, True)
            if both:
                outs[0][...] = jnp.concatenate(a + grad, axis=1)
            else:
                outs[0][...] = jnp.concatenate(a, axis=1)
                outs[1][...] = jnp.concatenate(grad, axis=1)

        return body

    wide = ((B, 4 * L),)
    (sent,) = call(back("y", 3, True, True), Y_TABLES, (exchange(sent), psi3, *column_all), wide)
    got3 = exchange(sent)
    sent, grad2 = call(back("x", 2, False, False), X_TABLES, (got3, psi2, *row_all), square)
    (sent,) = call(back("y", 1, False, True), Y_TABLES, (exchange(sent), psi1, *column_all), wide)
    got1 = exchange(sent)

    def final(tab, scalars, ins, outs):
        adj = propagate("x", parts_of(ins[0][...]), tab, True)
        grad0 = mul_conj(adj, parts_of(ins[1][...]))
        grads = (
            grad0,
            parts_of(ins[0][...], 2 * L),
            parts_of(ins[2][...]),
            parts_of(ins[3][...], 2 * L),
        )
        pos = lax.axis_index("section")
        for out, target_pos in ((outs[0], pos), (outs[1], pos + 1 - 2 * (pos % 2))):
            for part in range(2):
                value = grads[0][part]
                for layer in (1, 2, 3):
                    value = jnp.where(target_pos == layer, grads[layer][part], value)
                out[part] = collect(value)

    kept, given = call(
        final,
        X_TABLES,
        (got1, psi0, grad2, got3),
        ((2, T, N), (2, T, N)),
    )
    taken = lax.ppermute(given, "section", [(0, 1), (1, 0), (2, 3), (3, 2)])
    return (kept + taken)[None]


def solution(mesh):
    placed = (P("section", None, "row", None), P(None, "row", None), P(), P(None, "row", None))
    return jax.shard_map(
        shards,
        mesh=mesh,
        in_specs=placed,
        out_specs=P("section", None, "row", None),
        check_vma=False,
    )
```

```python
import math

import jax
import jax.numpy as jnp
import numpy as np
from jax import lax
from jax.experimental import pallas as pl
from jax.experimental.pallas import tpu as pltpu
from jax.sharding import PartitionSpec as P


N = 1024
B = 64
T = 16
L = T * T
fresnel_coef = 0.37
f32 = jnp.float32
bf16 = jnp.bfloat16


def split2(value):
    high = value.astype(bf16)
    return high, (value - high.astype(f32)).astype(bf16)


def np_split2(table):
    table = np.asarray(table, np.float64).astype(np.float32)
    high = table.astype(bf16)
    low = (table - high.astype(np.float32)).astype(bf16)
    return high, low


def left_table(cosine, sine):
    both = np.concatenate([cosine, sine], axis=0)
    high, low = np_split2(both)
    return np.concatenate([high, low, high], axis=1)


def pair(angle, scale=1.0):
    return np.stack([np.cos(angle), np.sin(angle)]).astype(np.float32) * np.float32(scale)


def complex_matrix(angle, scale):
    cosine, sine = np.cos(angle) * scale, np.sin(angle) * scale
    return np.concatenate(
        [np.concatenate([cosine, -sine], axis=1), np.concatenate([sine, cosine], axis=1)], axis=0
    )


def make_tables():
    two_pi = 2.0 * math.pi
    r32 = np.arange(32)
    r16 = np.arange(16)
    r8 = np.arange(8)
    blocks = np.arange(B)
    hb, ab = blocks // 32, blocks % 32
    lane_v, lane_t = np.repeat(r16, 16), np.tile(r16, 16)
    tab = {}
    angle = two_pi * np.outer(r32, r32) / 32
    eye2 = np.eye(2)
    tab["ly"] = left_table(np.kron(eye2, np.cos(angle)) / 8, np.kron(eye2, np.sin(angle)) / 8)
    tab["ty"] = pair(two_pi * (2 * lane_t[None, :] + hb[:, None]) * ab[:, None] / N)
    small = two_pi * np.outer(r16, r16) / 16
    mat = complex_matrix(small, 0.25)
    mat = mat.reshape(2, 16, 2, 16)
    full = np.einsum("atbk,vw->avtbwk", mat, np.eye(8)).reshape(256, 256)
    tab["ry"] = np.stack(np_split2(full))
    half = np.broadcast_to(two_pi * lane_t[None, :] / 32, (8, L))
    tab["by"] = pair(half)
    tab["by0"] = pair(np.broadcast_to(two_pi * lane_v[None, :] / 32, (8, L)))
    q = 2 * ab + hb
    angle = two_pi * np.outer(blocks, q) / B
    tab["lxf"] = left_table(np.cos(angle) / 8, np.sin(angle) / 8)
    tab["lxi"] = left_table(np.cos(angle.T) / 8, np.sin(angle.T) / 8)
    place = lane_v // 8 + 2 * (lane_v % 8)
    tab["tx"] = pair(two_pi * q[:, None] * place[None, :] / N)
    mat = complex_matrix(two_pi * np.outer(r8, r8) / 8, 0.25).reshape(2, 8, 2, 8)
    full = np.einsum("avbw,ts->avtbws", mat, np.eye(16)).reshape(256, 256)
    tab["rx"] = np.stack(np_split2(full))
    tab["bx"] = pair(np.broadcast_to(two_pi * np.repeat(r8, 16)[None, :] / 16, (8, 128)))
    signed = lambda freq: np.where(freq < N // 2, freq, freq - N).astype(np.float64)
    ky = ab[:, None] + 32 * lane_t[None, :] + 512 * hb[:, None]
    kx = 16 * blocks[:, None] + place[None, :]
    tab["hy"] = pair(-math.pi * fresnel_coef / N * signed(ky) ** 2)
    tab["hx"] = pair(-math.pi * fresnel_coef / N * signed(kx) ** 2)
    mat = complex_matrix(-small, 0.25).reshape(2, 16, 2, 16)
    order = np.zeros((16, 16))
    spot = np.arange(16)
    order[spot // 8 + 2 * (spot % 8), spot] = 1.0
    full = np.einsum("akbt,uw->akubwt", mat, order).reshape(512, 512)
    tab["ry0"] = np.stack(np_split2(full))
    tab["pm"] = np.einsum("kl,uw->kuwl", np.eye(16), order).reshape(256, 256).astype(bf16)
    return tab


def packed(tab):
    wide = lambda table: np.pad(np.asarray(table), ((0, 0), (0, L - table.shape[1])))
    rows = lambda parts: np.concatenate([wide(part) for part in parts], axis=0)
    both = lambda names: np.stack([rows([tab[n][part] for n in names]) for part in range(2)])
    return {
        "y16": rows([tab["ly"], tab["ry"][0], tab["ry"][1]]),
        "y32": both(("ty", "hy", "by")),
        "x16": rows([tab["lxf"], tab["lxi"], tab["rx"][0], tab["rx"][1], tab["pm"]]),
        "x32": both(("tx", "hx", "bx")),
        "first32": both(("ty", "by0")),
        "ry0": tab["ry0"],
        "ly": tab["ly"],
    }


TAB = packed(make_tables())


def mul(a, t):
    return a[0] * t[0] - a[1] * t[1], a[0] * t[1] + a[1] * t[0]


def mul_conj(a, t):
    return a[0] * t[0] + a[1] * t[1], a[1] * t[0] - a[0] * t[1]


def left(table, a, sign):
    high, low = split2(jnp.concatenate(a, axis=1))
    stacked = jnp.concatenate([high, high, low], axis=0)
    out = jnp.dot(table, stacked, preferred_element_type=f32)
    c_re, c_im, s_re, s_im = out[:B, :L], out[:B, L:], out[B:, :L], out[B:, L:]
    if sign > 0:
        return c_re + s_im, c_im - s_re
    return c_re - s_im, c_im + s_re


def times(data, table):
    rows = data.shape[0]
    high, low = split2(data)
    out = jnp.dot(jnp.concatenate([high, low], axis=0), table[0], preferred_element_type=f32)
    return out[:rows] + out[rows:] + jnp.dot(high, table[1], preferred_element_type=f32)


def right(table, a, sign):
    re, im = a
    if sign < 0:
        im = -im
    stacked = jnp.concatenate(
        [
            jnp.concatenate([re[:, :128], im[:, :128]], axis=1),
            jnp.concatenate([re[:, 128:], im[:, 128:]], axis=1),
        ],
        axis=0,
    )
    out = times(stacked, table)
    re = jnp.concatenate([out[:B, :128], out[B:, :128]], axis=1)
    im = jnp.concatenate([out[:B, 128:], out[B:, 128:]], axis=1)
    return (re, im) if sign > 0 else (re, -im)


def rows_join(a, b):
    return tuple(jnp.concatenate([x, y], axis=0) for x, y in zip(a, b))


def lanes_join(a, b):
    return tuple(jnp.concatenate([x, y], axis=1) for x, y in zip(a, b))


def plus(a, b):
    return a[0] + b[0], a[1] + b[1]


def minus(a, b):
    return a[0] - b[0], a[1] - b[1]


def y_forward(a, tab):
    a = left(tab["ly"], a, 1)
    a = mul_conj(a, tab["ty"])
    a = right(tab["ry"], a, 1)
    first = tuple(x[:32] for x in a)
    second = mul_conj(tuple(x[32:] for x in a), tuple(x[:1] for x in tab["by"]))
    return rows_join(plus(first, second), minus(first, second))


def y_unfold(a, turn):
    first, second = tuple(x[:32] for x in a), tuple(x[32:] for x in a)
    return plus(first, second), mul(minus(first, second), tuple(x[:1] for x in turn))


def y_inverse(a, tab):
    a = right(tab["ry"], rows_join(*y_unfold(a, tab["by"])), -1)
    a = mul(a, tab["ty"])
    return left(tab["ly"], a, -1)


def x_forward(a, tab):
    first, second = tuple(x[:, :128] for x in a), tuple(x[:, 128:] for x in a)
    turned = mul_conj(minus(first, second), tuple(x[:1] for x in tab["bx"]))
    a = right(tab["rx"], lanes_join(plus(first, second), turned), 1)
    a = mul_conj(a, tab["tx"])
    return left(tab["lxf"], a, 1)


def x_inverse(a, tab):
    a = left(tab["lxi"], a, -1)
    a = mul(a, tab["tx"])
    a = right(tab["rx"], a, -1)
    first = tuple(x[:, :128] for x in a)
    second = mul(tuple(x[:, 128:] for x in a), tuple(x[:1] for x in tab["bx"]))
    return lanes_join(plus(first, second), minus(first, second))


def spread(block):
    turned = block.T
    halves = [
        jnp.concatenate([turned[base + 32 * v : base + 32 * v + 32] for v in range(T)], axis=1)
        for base in (0, 512)
    ]
    return jnp.concatenate(halves, axis=0)


def collect(block):
    parts = [
        block[32 * h : 32 * h + 32, T * v : T * v + T] for h in range(2) for v in range(T)
    ]
    return jnp.concatenate(parts, axis=0).T


def unpacked(axis, small, large):
    tab = {}
    if axis == "y":
        tab["ly"] = small[0:128, 0:192]
        tab["ry"] = (small[128:384, :], small[384:640, :])
    else:
        tab["lxf"], tab["lxi"] = small[0:128, 0:192], small[128:256, 0:192]
        tab["rx"] = (small[256:512, :], small[512:768, :])
        tab["pm"] = small[768:1024, :]
    for name, at, lanes in (("t", slice(0, 64), L), ("h", slice(64, 128), L)):
        tab[name + axis] = tuple(large[part, at, 0:lanes] for part in range(2))
    lanes = L if axis == "y" else 128
    tab["b" + axis] = tuple(large[part, 128:136, 0:lanes] for part in range(2))
    return tab


def parts_of(value, at=0):
    return value[:, at : at + L], value[:, at + L : at + 2 * L]


def split3(value):
    high = value.astype(bf16)
    rest = value - high.astype(f32)
    middle = rest.astype(bf16)
    return jnp.concatenate([high, middle, (rest - middle.astype(f32)).astype(bf16)], axis=0)


def lanes_permuted(value, table):
    rows = value.shape[0]
    moved = jnp.dot(split3(value), table, preferred_element_type=f32)
    return moved[:rows] + (moved[rows : 2 * rows] + moved[2 * rows :])


def ramp_of(dy, dx, row_pos):
    lanes = lax.broadcasted_iota(jnp.int32, (8, N), 1)
    which = lax.broadcasted_iota(jnp.int32, (8, N), 0)
    turns = (lanes * dy - 256 * which) & (N - 1)
    wave = jnp.cos(turns.astype(f32) * f32(2.0 * math.pi / N))
    cos_y, sin_y = wave[0:1], wave[1:2]
    kx = lax.broadcasted_iota(jnp.int32, (T, 128), 0) + row_pos * T
    lane = lax.broadcasted_iota(jnp.int32, (T, 128), 1)
    turns = (kx * dx - 256 * lane) & (N - 1)
    wave = jnp.cos(turns.astype(f32) * f32(2.0 * math.pi / N))
    cos_x, sin_x = wave[:, 0:1], wave[:, 1:2]
    return cos_y * cos_x - sin_y * sin_x, cos_y * sin_x + sin_y * cos_x


def first_math(tab, probe, target, ramp):
    spec = tuple(spread(x) for x in mul_conj(probe, ramp))
    spec = rows_join(*y_unfold(spec, tab["by0"]))
    out = times(jnp.concatenate(spec, axis=1), tab["ry0"])
    field = left(tab["ly"], mul((out[:, :L], out[:, L:]), tab["ty"]), -1)
    return jnp.concatenate(field + (spread(target),), axis=1)


def forward_of(axis):
    return y_forward if axis == "y" else x_forward


def inverse_of(axis):
    return y_inverse if axis == "y" else x_inverse


def propagate(axis, a, tab, conj):
    spec = forward_of(axis)(a, tab)
    times_h = mul_conj if conj else mul
    return inverse_of(axis)(times_h(spec, tab["h" + axis]), tab)


FIRST_LIMIT = 61 * 1024 * 1024
VMEM_LIMIT = 16 * 1024 * 1024


def call(body, axis, operands, out_shapes):
    tables = [jnp.asarray(TAB[axis + bits]) for bits in ("16", "32")] if axis else []
    count = len(operands)

    def kernel(*refs):
        tab = unpacked(axis, *refs[count : count + 2]) if axis else {}
        body(tab, refs[:count], refs[count + len(tables) :])

    return pl.pallas_call(
        kernel,
        out_shape=[jax.ShapeDtypeStruct(shape, f32) for shape in out_shapes],
        in_specs=[pl.BlockSpec(memory_space=pltpu.VMEM)] * (count + len(tables)),
        out_specs=[pl.BlockSpec(memory_space=pltpu.VMEM)] * len(out_shapes),
        compiler_params=pltpu.CompilerParams(vmem_limit_bytes=VMEM_LIMIT),
    )(*operands, *tables)


def first_call(probe, target, offsets):
    names = ("ly", "first32", "ry0")

    def kernel(offsets_ref, probe_ref, target_ref, ly, small, ry0, out):
        wave = lax.axis_index("section") % 2
        tab = {"ly": ly[...], "ry0": (ry0[0], ry0[1])}
        tab["ty"] = (small[0, 0:64], small[1, 0:64])
        tab["by0"] = (small[0, 64:72], small[1, 64:72])
        ramp = ramp_of(offsets_ref[wave, 0], offsets_ref[wave, 1], lax.axis_index("row"))
        out[...] = first_math(
            tab,
            (probe_ref[0], probe_ref[1]),
            jnp.where(wave == 0, target_ref[0], target_ref[1]),
            ramp,
        )

    arrays = [probe, target] + [jnp.asarray(TAB[name]) for name in names]

    def whole(shape):
        return pl.BlockSpec(shape, lambda i: (0,) * len(shape))

    return pl.pallas_call(
        kernel,
        grid=(1,),
        out_shape=jax.ShapeDtypeStruct((B, 3 * L), f32),
        in_specs=[pl.BlockSpec((2, 2), lambda i: (0, 0), memory_space=pltpu.SMEM)]
        + [whole(a.shape) for a in arrays],
        out_specs=whole((B, 3 * L)),
        compiler_params=pltpu.CompilerParams(vmem_limit_bytes=FIRST_LIMIT),
    )(offsets, *arrays)


def exchange(value):
    return lax.all_to_all(value, "row", split_axis=0, concat_axis=0, tiled=True)


def shards(object_slices, probe_spec, offsets, measured):
    own = object_slices[0]
    raw = [lax.ppermute(own, "section", [(s, (s + k) % 4) for s in range(4)]) for k in (1, 2, 3)]
    sent, *raw = lax.optimization_barrier((first_call(probe_spec, measured, offsets), *raw))
    got1 = exchange(sent)

    def arrange(tab, ins, outs):
        place = lax.axis_index("section")
        for layer in range(4):
            turn = (place - layer) % 4
            for part in range(2):
                value = ins[0][part]
                for k in (1, 2, 3):
                    value = jnp.where(turn == k, ins[k][part], value)
                outs[layer][:, part * L : part * L + L] = spread(value)

    obj = call(arrange, "", (own, *raw), ((B, 2 * L),) * 4)

    def second(tab, ins, outs):
        value = ins[0][...]
        psi = x_inverse(parts_of(value), tab)
        outs[0][...] = jnp.concatenate(psi, axis=1)
        a = propagate("x", mul(psi, parts_of(ins[1][...])), tab, False)
        outs[1][...] = jnp.concatenate(a + (ins[2][...],), axis=1)
        outs[2][...] = lanes_permuted(value[:, 2 * L :], tab["pm"])

    psi0, sent, target = call(
        second,
        "x",
        (got1, obj[0], obj[1]),
        ((B, 2 * L), (B, 4 * L), (B, L)),
    )

    def third(tab, ins, outs):
        value = ins[0][...]
        psi = propagate("y", parts_of(value), tab, False)
        outs[0][...] = jnp.concatenate(psi, axis=1)
        a = propagate("y", mul(psi, parts_of(value, 2 * L)), tab, False)
        outs[1][...] = jnp.concatenate(a, axis=1)

    got2 = exchange(sent)
    psi1, sent = call(third, "y", (got2,), ((B, 2 * L),) * 2)

    def fourth(tab, ins, outs):
        psi = propagate("x", parts_of(ins[0][...]), tab, False)
        outs[0][...] = jnp.concatenate(psi, axis=1)
        a = propagate("x", mul(psi, parts_of(ins[1][...])), tab, False)
        outs[1][...] = jnp.concatenate(a + (ins[2][...],), axis=1)

    psi2, sent = call(
        fourth, "x", (exchange(sent), obj[2], obj[3]), ((B, 2 * L), (B, 4 * L))
    )

    def fifth(tab, ins, outs):
        value = ins[0][...]
        psi = propagate("y", parts_of(value), tab, False)
        outs[0][...] = jnp.concatenate(psi, axis=1)
        a = y_forward(mul(psi, parts_of(value, 2 * L)), tab)
        outs[1][...] = jnp.concatenate(a, axis=1)

    got4 = exchange(sent)
    psi3, sent = call(fifth, "y", (got4,), ((B, 2 * L),) * 2)

    def far(tab, ins, outs):
        phi = x_forward(parts_of(ins[0][...]), tab)
        weight = 0.5 * (phi[0] * phi[0] + phi[1] * phi[1] - ins[1][...])
        a = x_inverse((phi[0] * weight, phi[1] * weight), tab)
        outs[0][...] = jnp.concatenate(a, axis=1)

    (sent,) = call(far, "x", (exchange(sent), target), ((B, 2 * L),))

    def back_third(tab, ins, outs):
        adj = y_inverse(parts_of(ins[0][...]), tab)
        grad = mul_conj(adj, parts_of(ins[1][...]))
        a = propagate("y", mul_conj(adj, parts_of(ins[2][...], 2 * L)), tab, True)
        outs[0][...] = jnp.concatenate(a, axis=1)
        outs[1][...] = jnp.concatenate(grad, axis=1)

    square = ((B, 2 * L),) * 2
    sent, grad3 = call(back_third, "y", (exchange(sent), psi3, got4), square)

    def back_second(tab, ins, outs):
        adj = propagate("x", parts_of(ins[0][...]), tab, True)
        grad = mul_conj(adj, parts_of(ins[1][...]))
        a = propagate("x", mul_conj(adj, parts_of(ins[2][...])), tab, True)
        outs[0][...] = jnp.concatenate(a, axis=1)
        outs[1][...] = jnp.concatenate(grad, axis=1)

    sent, grad2 = call(back_second, "x", (exchange(sent), psi2, obj[2]), square)

    def back_first(tab, ins, outs):
        adj = propagate("y", parts_of(ins[0][...]), tab, True)
        grad = mul_conj(adj, parts_of(ins[1][...]))
        a = propagate("y", mul_conj(adj, parts_of(ins[2][...], 2 * L)), tab, True)
        ride = jnp.where(lax.axis_index("section") < 2, jnp.concatenate(grad, axis=1), ins[3][...])
        outs[0][...] = jnp.concatenate(a + (ride,), axis=1)

    (sent,) = call(
        back_first, "y", (exchange(sent), psi1, got2, grad3), ((B, 4 * L),)
    )

    def last(tab, ins, outs):
        value = ins[0][...]
        adj = propagate("x", parts_of(value), tab, True)
        grad = mul_conj(adj, parts_of(ins[1][...]))
        pos = lax.axis_index("section")
        other = parts_of(ins[2][...])
        upper = parts_of(value, 2 * L)
        for part in range(2):
            lower = jnp.where(pos < 2, grad[part], other[part])
            outs[0][part] = collect(jnp.where(pos % 2 == 0, lower, upper[part]))
            outs[1][part] = collect(jnp.where(pos % 2 == 0, upper[part], lower))

    kept, given = call(last, "x", (exchange(sent), psi0, grad2), ((2, T, N),) * 2)
    taken = lax.ppermute(given, "section", [(0, 1), (1, 0), (2, 3), (3, 2)])
    return (kept + taken)[None]


def solution(mesh):
    placed = (P("section", None, "row", None), P(None, "row", None), P(), P(None, "row", None))
    return jax.shard_map(
        shards,
        mesh=mesh,
        in_specs=placed,
        out_specs=P("section", None, "row", None),
        check_vma=False,
    )
```

```python
import math

import jax
import jax.numpy as jnp
import numpy as np
from jax import lax
from jax.experimental import pallas as pl
from jax.experimental.pallas import tpu as pltpu
from jax.sharding import PartitionSpec as P


N = 1024
B = 64
T = 16
L = T * T
fresnel_coef = 0.37
f32 = jnp.float32
bf16 = jnp.bfloat16


def split2(value):
    high = value.astype(bf16)
    return high, (value - high.astype(f32)).astype(bf16)


def np_split2(table):
    table = np.asarray(table, np.float64).astype(np.float32)
    high = table.astype(bf16)
    low = (table - high.astype(np.float32)).astype(bf16)
    return high, low


def left_table(cosine, sine):
    both = np.concatenate([cosine, sine], axis=0)
    high, low = np_split2(both)
    return np.concatenate([high, low, high], axis=1)


def pair(angle, scale=1.0):
    return np.stack([np.cos(angle), np.sin(angle)]).astype(np.float32) * np.float32(scale)


def complex_matrix(angle, scale):
    cosine, sine = np.cos(angle) * scale, np.sin(angle) * scale
    return np.concatenate(
        [np.concatenate([cosine, -sine], axis=1), np.concatenate([sine, cosine], axis=1)], axis=0
    )


def make_tables():
    two_pi = 2.0 * math.pi
    r32 = np.arange(32)
    r16 = np.arange(16)
    r8 = np.arange(8)
    blocks = np.arange(B)
    hb, ab = blocks // 32, blocks % 32
    lane_v, lane_t = np.repeat(r16, 16), np.tile(r16, 16)
    tab = {}
    angle = two_pi * np.outer(r32, r32) / 32
    eye2 = np.eye(2)
    tab["ly"] = left_table(np.kron(eye2, np.cos(angle)) / 8, np.kron(eye2, np.sin(angle)) / 8)
    tab["ty"] = pair(two_pi * (2 * lane_t[None, :] + hb[:, None]) * ab[:, None] / N)
    small = two_pi * np.outer(r16, r16) / 16
    mat = complex_matrix(small, 0.25)
    mat = mat.reshape(2, 16, 2, 16)
    full = np.einsum("atbk,vw->avtbwk", mat, np.eye(8)).reshape(256, 256)
    tab["ry"] = np.stack(np_split2(full))
    half = np.broadcast_to(two_pi * lane_t[None, :] / 32, (8, L))
    tab["by"] = pair(half)
    tab["by0"] = pair(np.broadcast_to(two_pi * lane_v[None, :] / 32, (8, L)))
    q = 2 * ab + hb
    angle = two_pi * np.outer(blocks, q) / B
    tab["lxf"] = left_table(np.cos(angle) / 8, np.sin(angle) / 8)
    tab["lxi"] = left_table(np.cos(angle.T) / 8, np.sin(angle.T) / 8)
    place = lane_v // 8 + 2 * (lane_v % 8)
    tab["tx"] = pair(two_pi * q[:, None] * place[None, :] / N)
    mat = complex_matrix(two_pi * np.outer(r8, r8) / 8, 0.25).reshape(2, 8, 2, 8)
    full = np.einsum("avbw,ts->avtbws", mat, np.eye(16)).reshape(256, 256)
    tab["rx"] = np.stack(np_split2(full))
    tab["bx"] = pair(np.broadcast_to(two_pi * np.repeat(r8, 16)[None, :] / 16, (8, 128)))
    signed = lambda freq: np.where(freq < N // 2, freq, freq - N).astype(np.float64)
    ky = ab[:, None] + 32 * lane_t[None, :] + 512 * hb[:, None]
    kx = 16 * blocks[:, None] + place[None, :]
    tab["hy"] = pair(-math.pi * fresnel_coef / N * signed(ky) ** 2)
    tab["hx"] = pair(-math.pi * fresnel_coef / N * signed(kx) ** 2)
    mat = complex_matrix(-small, 0.25).reshape(2, 16, 2, 16)
    order = np.zeros((16, 16))
    spot = np.arange(16)
    order[spot // 8 + 2 * (spot % 8), spot] = 1.0
    full = np.einsum("akbt,uw->akubwt", mat, order).reshape(512, 512)
    tab["ry0"] = np.stack(np_split2(full))
    tab["pm"] = np.einsum("kl,uw->kuwl", np.eye(16), order).reshape(256, 256).astype(bf16)
    return tab


def packed(tab):
    wide = lambda table: np.pad(np.asarray(table), ((0, 0), (0, L - table.shape[1])))
    rows = lambda parts: np.concatenate([wide(part) for part in parts], axis=0)
    both = lambda names: np.stack([rows([tab[n][part] for n in names]) for part in range(2)])
    return {
        "y16": rows([tab["ly"], tab["ry"][0], tab["ry"][1]]),
        "y32": both(("ty", "hy", "by")),
        "x16": rows([tab["lxf"], tab["lxi"], tab["rx"][0], tab["rx"][1], tab["pm"]]),
        "x32": both(("tx", "hx", "bx")),
        "first32": both(("ty", "by0")),
        "ry0": tab["ry0"],
        "ly": tab["ly"],
    }


TAB = packed(make_tables())


def wide(ref):
    count = ref.shape[0] // B
    return jnp.concatenate(
        [ref[pl.ds(i, B, stride=count), :] for i in range(count)], axis=1
    )


def put(ref, value):
    count = ref.shape[0] // B
    for i in range(count):
        ref[pl.ds(i, B, stride=count), :] = value[:, 128 * i : 128 * i + 128]


def mul(a, t):
    return a[0] * t[0] - a[1] * t[1], a[0] * t[1] + a[1] * t[0]


def mul_conj(a, t):
    return a[0] * t[0] + a[1] * t[1], a[1] * t[0] - a[0] * t[1]


def left(table, a, sign):
    high, low = split2(jnp.concatenate(a, axis=1))
    stacked = jnp.concatenate([high, high, low], axis=0)
    out = jnp.dot(table, stacked, preferred_element_type=f32)
    c_re, c_im, s_re, s_im = out[:B, :L], out[:B, L:], out[B:, :L], out[B:, L:]
    if sign > 0:
        return c_re + s_im, c_im - s_re
    return c_re - s_im, c_im + s_re


def times(data, table):
    rows = data.shape[0]
    high, low = split2(data)
    out = jnp.dot(jnp.concatenate([high, low], axis=0), table[0], preferred_element_type=f32)
    return out[:rows] + out[rows:] + jnp.dot(high, table[1], preferred_element_type=f32)


def right(table, a, sign):
    re, im = a
    if sign < 0:
        im = -im
    stacked = jnp.concatenate(
        [
            jnp.concatenate([re[:, :128], im[:, :128]], axis=1),
            jnp.concatenate([re[:, 128:], im[:, 128:]], axis=1),
        ],
        axis=0,
    )
    out = times(stacked, table)
    re = jnp.concatenate([out[:B, :128], out[B:, :128]], axis=1)
    im = jnp.concatenate([out[:B, 128:], out[B:, 128:]], axis=1)
    return (re, im) if sign > 0 else (re, -im)


def rows_join(a, b):
    return tuple(jnp.concatenate([x, y], axis=0) for x, y in zip(a, b))


def lanes_join(a, b):
    return tuple(jnp.concatenate([x, y], axis=1) for x, y in zip(a, b))


def plus(a, b):
    return a[0] + b[0], a[1] + b[1]


def minus(a, b):
    return a[0] - b[0], a[1] - b[1]


def y_forward(a, tab):
    a = left(tab["ly"], a, 1)
    a = mul_conj(a, tab["ty"])
    a = right(tab["ry"], a, 1)
    first = tuple(x[:32] for x in a)
    second = mul_conj(tuple(x[32:] for x in a), tuple(x[:1] for x in tab["by"]))
    return rows_join(plus(first, second), minus(first, second))


def y_unfold(a, turn):
    first, second = tuple(x[:32] for x in a), tuple(x[32:] for x in a)
    return plus(first, second), mul(minus(first, second), tuple(x[:1] for x in turn))


def y_inverse(a, tab):
    a = right(tab["ry"], rows_join(*y_unfold(a, tab["by"])), -1)
    a = mul(a, tab["ty"])
    return left(tab["ly"], a, -1)


def x_forward(a, tab):
    first, second = tuple(x[:, :128] for x in a), tuple(x[:, 128:] for x in a)
    turned = mul_conj(minus(first, second), tuple(x[:1] for x in tab["bx"]))
    a = right(tab["rx"], lanes_join(plus(first, second), turned), 1)
    a = mul_conj(a, tab["tx"])
    return left(tab["lxf"], a, 1)


def x_inverse(a, tab):
    a = left(tab["lxi"], a, -1)
    a = mul(a, tab["tx"])
    a = right(tab["rx"], a, -1)
    first = tuple(x[:, :128] for x in a)
    second = mul(tuple(x[:, 128:] for x in a), tuple(x[:1] for x in tab["bx"]))
    return lanes_join(plus(first, second), minus(first, second))


def spread(block):
    turned = block.T
    halves = [
        jnp.concatenate([turned[base + 32 * v : base + 32 * v + 32] for v in range(T)], axis=1)
        for base in (0, 512)
    ]
    return jnp.concatenate(halves, axis=0)


def collect(block):
    parts = [
        block[32 * h : 32 * h + 32, T * v : T * v + T] for h in range(2) for v in range(T)
    ]
    return jnp.concatenate(parts, axis=0).T


def unpacked(axis, small, large):
    tab = {}
    if axis == "y":
        tab["ly"] = small[0:128, 0:192]
        tab["ry"] = (small[128:384, :], small[384:640, :])
    else:
        tab["lxf"], tab["lxi"] = small[0:128, 0:192], small[128:256, 0:192]
        tab["rx"] = (small[256:512, :], small[512:768, :])
        tab["pm"] = small[768:1024, :]
    for name, at, lanes in (("t", slice(0, 64), L), ("h", slice(64, 128), L)):
        tab[name + axis] = tuple(large[part, at, 0:lanes] for part in range(2))
    lanes = L if axis == "y" else 128
    tab["b" + axis] = tuple(large[part, 128:136, 0:lanes] for part in range(2))
    return tab


def parts_of(value, at=0):
    return value[:, at : at + L], value[:, at + L : at + 2 * L]


def split3(value):
    high = value.astype(bf16)
    rest = value - high.astype(f32)
    middle = rest.astype(bf16)
    return jnp.concatenate([high, middle, (rest - middle.astype(f32)).astype(bf16)], axis=0)


def lanes_permuted(value, table):
    rows = value.shape[0]
    moved = jnp.dot(split3(value), table, preferred_element_type=f32)
    return moved[:rows] + (moved[rows : 2 * rows] + moved[2 * rows :])


def ramp_of(dy, dx, row_pos):
    lanes = lax.broadcasted_iota(jnp.int32, (8, N), 1)
    which = lax.broadcasted_iota(jnp.int32, (8, N), 0)
    turns = (lanes * dy - 256 * which) & (N - 1)
    wave = jnp.cos(turns.astype(f32) * f32(2.0 * math.pi / N))
    cos_y, sin_y = wave[0:1], wave[1:2]
    kx = lax.broadcasted_iota(jnp.int32, (T, 128), 0) + row_pos * T
    lane = lax.broadcasted_iota(jnp.int32, (T, 128), 1)
    turns = (kx * dx - 256 * lane) & (N - 1)
    wave = jnp.cos(turns.astype(f32) * f32(2.0 * math.pi / N))
    cos_x, sin_x = wave[:, 0:1], wave[:, 1:2]
    return cos_y * cos_x - sin_y * sin_x, cos_y * sin_x + sin_y * cos_x


def first_math(tab, probe, target, ramp):
    spec = tuple(spread(x) for x in mul_conj(probe, ramp))
    spec = rows_join(*y_unfold(spec, tab["by0"]))
    out = times(jnp.concatenate(spec, axis=1), tab["ry0"])
    field = left(tab["ly"], mul((out[:, :L], out[:, L:]), tab["ty"]), -1)
    return jnp.concatenate(field + (spread(target), jnp.zeros((B, L), f32)), axis=1)


def forward_of(axis):
    return y_forward if axis == "y" else x_forward


def inverse_of(axis):
    return y_inverse if axis == "y" else x_inverse


def propagate(axis, a, tab, conj):
    spec = forward_of(axis)(a, tab)
    times_h = mul_conj if conj else mul
    return inverse_of(axis)(times_h(spec, tab["h" + axis]), tab)


FIRST_LIMIT = 61 * 1024 * 1024
VMEM_LIMIT = 16 * 1024 * 1024


def call(body, axis, operands, out_shapes):
    tables = [jnp.asarray(TAB[axis + bits]) for bits in ("16", "32")] if axis else []
    count = len(operands)

    def kernel(*refs):
        tab = unpacked(axis, *refs[count : count + 2]) if axis else {}
        body(tab, refs[:count], refs[count + len(tables) :])

    return pl.pallas_call(
        kernel,
        out_shape=[jax.ShapeDtypeStruct(shape, f32) for shape in out_shapes],
        in_specs=[pl.BlockSpec(memory_space=pltpu.VMEM)] * (count + len(tables)),
        out_specs=[pl.BlockSpec(memory_space=pltpu.VMEM)] * len(out_shapes),
        compiler_params=pltpu.CompilerParams(vmem_limit_bytes=VMEM_LIMIT),
    )(*operands, *tables)


def first_call(probe, target, offsets):
    names = ("ly", "first32", "ry0")

    def kernel(offsets_ref, probe_ref, target_ref, ly, small, ry0, out):
        wave = lax.axis_index("section") % 2
        tab = {"ly": ly[...], "ry0": (ry0[0], ry0[1])}
        tab["ty"] = (small[0, 0:64], small[1, 0:64])
        tab["by0"] = (small[0, 64:72], small[1, 64:72])
        ramp = ramp_of(offsets_ref[wave, 0], offsets_ref[wave, 1], lax.axis_index("row"))
        value = first_math(
            tab,
            (probe_ref[0], probe_ref[1]),
            jnp.where(wave == 0, target_ref[0], target_ref[1]),
            ramp,
        )
        put(out, value)

    arrays = [probe, target] + [jnp.asarray(TAB[name]) for name in names]

    def whole(shape):
        return pl.BlockSpec(shape, lambda i: (0,) * len(shape))

    return pl.pallas_call(
        kernel,
        grid=(1,),
        out_shape=jax.ShapeDtypeStruct((8 * B, 128), f32),
        in_specs=[pl.BlockSpec((2, 2), lambda i: (0, 0), memory_space=pltpu.SMEM)]
        + [whole(a.shape) for a in arrays],
        out_specs=whole((8 * B, 128)),
        compiler_params=pltpu.CompilerParams(vmem_limit_bytes=FIRST_LIMIT),
    )(offsets, *arrays)


def exchange(value):
    return lax.all_to_all(value, "row", split_axis=0, concat_axis=0, tiled=True)


def shards(object_slices, probe_spec, offsets, measured):
    own = object_slices[0]
    raw = [lax.ppermute(own, "section", [(s, (s + k) % 4) for s in range(4)]) for k in (1, 2, 3)]
    sent, *raw = lax.optimization_barrier((first_call(probe_spec, measured, offsets), *raw))
    got1 = exchange(sent)

    def arrange(tab, ins, outs):
        place = lax.axis_index("section")
        for layer in range(4):
            turn = (place - layer) % 4
            for part in range(2):
                value = ins[0][part]
                for k in (1, 2, 3):
                    value = jnp.where(turn == k, ins[k][part], value)
                outs[layer][:, part * L : part * L + L] = spread(value)

    obj = call(arrange, "", (own, *raw), ((B, 2 * L),) * 4)

    def second(tab, ins, outs):
        value = wide(ins[0])
        psi = x_inverse(parts_of(value), tab)
        outs[0][...] = jnp.concatenate(psi, axis=1)
        a = propagate("x", mul(psi, parts_of(ins[1][...])), tab, False)
        put(outs[1], jnp.concatenate(a + (ins[2][...],), axis=1))
        outs[2][...] = lanes_permuted(value[:, 2 * L : 3 * L], tab["pm"])

    psi0, sent, target = call(
        second,
        "x",
        (got1, obj[0], obj[1]),
        ((B, 2 * L), (8 * B, 128), (B, L)),
    )

    def third(tab, ins, outs):
        value = wide(ins[0])
        psi = propagate("y", parts_of(value), tab, False)
        outs[0][...] = jnp.concatenate(psi, axis=1)
        a = propagate("y", mul(psi, parts_of(value, 2 * L)), tab, False)
        put(outs[1], jnp.concatenate(a, axis=1))

    got2 = exchange(sent)
    psi1, sent = call(third, "y", (got2,), ((B, 2 * L), (4 * B, 128)))

    def fourth(tab, ins, outs):
        psi = propagate("x", parts_of(wide(ins[0])), tab, False)
        outs[0][...] = jnp.concatenate(psi, axis=1)
        a = propagate("x", mul(psi, parts_of(ins[1][...])), tab, False)
        put(outs[1], jnp.concatenate(a + (ins[2][...],), axis=1))

    psi2, sent = call(
        fourth, "x", (exchange(sent), obj[2], obj[3]), ((B, 2 * L), (8 * B, 128))
    )

    def fifth(tab, ins, outs):
        value = wide(ins[0])
        psi = propagate("y", parts_of(value), tab, False)
        outs[0][...] = jnp.concatenate(psi, axis=1)
        a = y_forward(mul(psi, parts_of(value, 2 * L)), tab)
        put(outs[1], jnp.concatenate(a, axis=1))

    got4 = exchange(sent)
    psi3, sent = call(fifth, "y", (got4,), ((B, 2 * L), (4 * B, 128)))

    def far(tab, ins, outs):
        phi = x_forward(parts_of(wide(ins[0])), tab)
        weight = 0.5 * (phi[0] * phi[0] + phi[1] * phi[1] - ins[1][...])
        a = x_inverse((phi[0] * weight, phi[1] * weight), tab)
        put(outs[0], jnp.concatenate(a, axis=1))

    (sent,) = call(far, "x", (exchange(sent), target), ((4 * B, 128),))

    def back_third(tab, ins, outs):
        adj = y_inverse(parts_of(wide(ins[0])), tab)
        grad = mul_conj(adj, parts_of(ins[1][...]))
        a = propagate("y", mul_conj(adj, parts_of(wide(ins[2]), 2 * L)), tab, True)
        put(outs[0], jnp.concatenate(a, axis=1))
        outs[1][...] = jnp.concatenate(grad, axis=1)

    square = ((4 * B, 128), (B, 2 * L))
    sent, grad3 = call(back_third, "y", (exchange(sent), psi3, got4), square)

    def back_second(tab, ins, outs):
        adj = propagate("x", parts_of(wide(ins[0])), tab, True)
        grad = mul_conj(adj, parts_of(ins[1][...]))
        a = propagate("x", mul_conj(adj, parts_of(ins[2][...])), tab, True)
        put(outs[0], jnp.concatenate(a, axis=1))
        outs[1][...] = jnp.concatenate(grad, axis=1)

    sent, grad2 = call(back_second, "x", (exchange(sent), psi2, obj[2]), square)

    def back_first(tab, ins, outs):
        adj = propagate("y", parts_of(wide(ins[0])), tab, True)
        grad = mul_conj(adj, parts_of(ins[1][...]))
        a = propagate("y", mul_conj(adj, parts_of(wide(ins[2]), 2 * L)), tab, True)
        ride = jnp.where(lax.axis_index("section") < 2, jnp.concatenate(grad, axis=1), ins[3][...])
        put(outs[0], jnp.concatenate(a + (ride,), axis=1))

    (sent,) = call(
        back_first, "y", (exchange(sent), psi1, got2, grad3), ((8 * B, 128),)
    )

    def last(tab, ins, outs):
        value = wide(ins[0])
        adj = propagate("x", parts_of(value), tab, True)
        grad = mul_conj(adj, parts_of(ins[1][...]))
        pos = lax.axis_index("section")
        other = parts_of(ins[2][...])
        upper = parts_of(value, 2 * L)
        for part in range(2):
            lower = jnp.where(pos < 2, grad[part], other[part])
            outs[0][part] = collect(jnp.where(pos % 2 == 0, lower, upper[part]))
            outs[1][part] = collect(jnp.where(pos % 2 == 0, upper[part], lower))

    kept, given = call(last, "x", (exchange(sent), psi0, grad2), ((2, T, N),) * 2)
    taken = lax.ppermute(given, "section", [(0, 1), (1, 0), (2, 3), (3, 2)])
    return (kept + taken)[None]


def solution(mesh):
    placed = (P("section", None, "row", None), P(None, "row", None), P(), P(None, "row", None))
    return jax.shard_map(
        shards,
        mesh=mesh,
        in_specs=placed,
        out_specs=P("section", None, "row", None),
        check_vma=False,
    )
```

```python
import math

import jax
import jax.numpy as jnp
import numpy as np
from jax import lax
from jax.experimental import pallas as pl
from jax.experimental.pallas import tpu as pltpu
from jax.sharding import PartitionSpec as P


N = 1024
B = 64
T = 16
L = T * T
fresnel_coef = 0.37
f32 = jnp.float32
bf16 = jnp.bfloat16


def split2(value):
    high = value.astype(bf16)
    return high, (value - high.astype(f32)).astype(bf16)


def np_split2(table):
    table = np.asarray(table, np.float64).astype(np.float32)
    high = table.astype(bf16)
    low = (table - high.astype(np.float32)).astype(bf16)
    return high, low


def left_table(cosine, sine):
    both = np.concatenate([cosine, sine], axis=0)
    high, low = np_split2(both)
    return np.concatenate([high, low, high], axis=1)


def pair(angle, scale=1.0):
    return np.stack([np.cos(angle), np.sin(angle)]).astype(np.float32) * np.float32(scale)


def complex_matrix(angle, scale):
    cosine, sine = np.cos(angle) * scale, np.sin(angle) * scale
    return np.concatenate(
        [np.concatenate([cosine, -sine], axis=1), np.concatenate([sine, cosine], axis=1)], axis=0
    )


def make_tables():
    two_pi = 2.0 * math.pi
    r32 = np.arange(32)
    r16 = np.arange(16)
    r8 = np.arange(8)
    blocks = np.arange(B)
    hb, ab = blocks // 32, blocks % 32
    lane_v, lane_t = np.repeat(r16, 16), np.tile(r16, 16)
    tab = {}
    angle = two_pi * np.outer(r32, r32) / 32
    eye2 = np.eye(2)
    tab["ly"] = left_table(np.kron(eye2, np.cos(angle)) / 8, np.kron(eye2, np.sin(angle)) / 8)
    tab["ty"] = pair(two_pi * (2 * lane_t[None, :] + hb[:, None]) * ab[:, None] / N)
    small = two_pi * np.outer(r16, r16) / 16
    mat = complex_matrix(small, 0.25)
    mat = mat.reshape(2, 16, 2, 16)
    full = np.einsum("atbk,vw->avtbwk", mat, np.eye(8)).reshape(256, 256)
    tab["ry"] = np.stack(np_split2(full))
    half = np.broadcast_to(two_pi * lane_t[None, :] / 32, (8, L))
    tab["by"] = pair(half)
    tab["by0"] = pair(np.broadcast_to(two_pi * lane_v[None, :] / 32, (8, L)))
    q = 2 * ab + hb
    angle = two_pi * np.outer(blocks, q) / B
    tab["lxf"] = left_table(np.cos(angle) / 8, np.sin(angle) / 8)
    tab["lxi"] = left_table(np.cos(angle.T) / 8, np.sin(angle.T) / 8)
    place = lane_v // 8 + 2 * (lane_v % 8)
    tab["tx"] = pair(two_pi * q[:, None] * place[None, :] / N)
    mat = complex_matrix(two_pi * np.outer(r8, r8) / 8, 0.25).reshape(2, 8, 2, 8)
    full = np.einsum("avbw,ts->avtbws", mat, np.eye(16)).reshape(256, 256)
    tab["rx"] = np.stack(np_split2(full))
    tab["bx"] = pair(np.broadcast_to(two_pi * np.repeat(r8, 16)[None, :] / 16, (8, 128)))
    signed = lambda freq: np.where(freq < N // 2, freq, freq - N).astype(np.float64)
    ky = ab[:, None] + 32 * lane_t[None, :] + 512 * hb[:, None]
    kx = 16 * blocks[:, None] + place[None, :]
    tab["hy"] = pair(-math.pi * fresnel_coef / N * signed(ky) ** 2)
    tab["hx"] = pair(-math.pi * fresnel_coef / N * signed(kx) ** 2)
    mat = complex_matrix(-small, 0.25).reshape(2, 16, 2, 16)
    order = np.zeros((16, 16))
    spot = np.arange(16)
    order[spot // 8 + 2 * (spot % 8), spot] = 1.0
    full = np.einsum("akbt,uw->akubwt", mat, order).reshape(512, 512)
    tab["ry0"] = np.stack(np_split2(full))
    tab["pm"] = np.einsum("kl,uw->kuwl", np.eye(16), order).reshape(256, 256).astype(bf16)
    return tab


def packed(tab):
    wide = lambda table: np.pad(np.asarray(table), ((0, 0), (0, L - table.shape[1])))
    rows = lambda parts: np.concatenate([wide(part) for part in parts], axis=0)
    both = lambda names: np.stack([rows([tab[n][part] for n in names]) for part in range(2)])
    return {
        "y16": rows([tab["ly"], tab["ry"][0], tab["ry"][1]]),
        "y32": both(("ty", "hy", "by")),
        "x16": rows([tab["lxf"], tab["lxi"], tab["rx"][0], tab["rx"][1]]),
        "x32": both(("tx", "hx", "bx")),
        "first32": both(("ty", "by0")),
        "ry0": tab["ry0"],
        "ly": tab["ly"],
        "pm": tab["pm"],
    }


TAB = packed(make_tables())


def wide(ref):
    count = ref.shape[0] // B
    return jnp.concatenate(
        [ref[pl.ds(i, B, stride=count), :] for i in range(count)], axis=1
    )


def put(ref, value):
    count = ref.shape[0] // B
    for i in range(count):
        ref[pl.ds(i, B, stride=count), :] = value[:, 128 * i : 128 * i + 128]


def mul(a, t):
    return a[0] * t[0] - a[1] * t[1], a[0] * t[1] + a[1] * t[0]


def mul_conj(a, t):
    return a[0] * t[0] + a[1] * t[1], a[1] * t[0] - a[0] * t[1]


def left(table, a, sign):
    high, low = split2(jnp.concatenate(a, axis=1))
    stacked = jnp.concatenate([high, high, low], axis=0)
    out = jnp.dot(table, stacked, preferred_element_type=f32)
    c_re, c_im, s_re, s_im = out[:B, :L], out[:B, L:], out[B:, :L], out[B:, L:]
    if sign > 0:
        return c_re + s_im, c_im - s_re
    return c_re - s_im, c_im + s_re


def times(data, table):
    rows = data.shape[0]
    high, low = split2(data)
    out = jnp.dot(jnp.concatenate([high, low], axis=0), table[0], preferred_element_type=f32)
    return out[:rows] + out[rows:] + jnp.dot(high, table[1], preferred_element_type=f32)


def right(table, a, sign):
    re, im = a
    if sign < 0:
        im = -im
    stacked = jnp.concatenate(
        [
            jnp.concatenate([re[:, :128], im[:, :128]], axis=1),
            jnp.concatenate([re[:, 128:], im[:, 128:]], axis=1),
        ],
        axis=0,
    )
    out = times(stacked, table)
    re = jnp.concatenate([out[:B, :128], out[B:, :128]], axis=1)
    im = jnp.concatenate([out[:B, 128:], out[B:, 128:]], axis=1)
    return (re, im) if sign > 0 else (re, -im)


def rows_join(a, b):
    return tuple(jnp.concatenate([x, y], axis=0) for x, y in zip(a, b))


def lanes_join(a, b):
    return tuple(jnp.concatenate([x, y], axis=1) for x, y in zip(a, b))


def plus(a, b):
    return a[0] + b[0], a[1] + b[1]


def minus(a, b):
    return a[0] - b[0], a[1] - b[1]


def y_forward(a, tab):
    a = left(tab["ly"], a, 1)
    a = mul_conj(a, tab["ty"])
    a = right(tab["ry"], a, 1)
    first = tuple(x[:32] for x in a)
    second = mul_conj(tuple(x[32:] for x in a), tuple(x[:1] for x in tab["by"]))
    return rows_join(plus(first, second), minus(first, second))


def y_unfold(a, turn):
    first, second = tuple(x[:32] for x in a), tuple(x[32:] for x in a)
    return plus(first, second), mul(minus(first, second), tuple(x[:1] for x in turn))


def y_inverse(a, tab):
    a = right(tab["ry"], rows_join(*y_unfold(a, tab["by"])), -1)
    a = mul(a, tab["ty"])
    return left(tab["ly"], a, -1)


def x_forward(a, tab):
    first, second = tuple(x[:, :128] for x in a), tuple(x[:, 128:] for x in a)
    turned = mul_conj(minus(first, second), tuple(x[:1] for x in tab["bx"]))
    a = right(tab["rx"], lanes_join(plus(first, second), turned), 1)
    a = mul_conj(a, tab["tx"])
    return left(tab["lxf"], a, 1)


def x_inverse(a, tab):
    a = left(tab["lxi"], a, -1)
    a = mul(a, tab["tx"])
    a = right(tab["rx"], a, -1)
    first = tuple(x[:, :128] for x in a)
    second = mul(tuple(x[:, 128:] for x in a), tuple(x[:1] for x in tab["bx"]))
    return lanes_join(plus(first, second), minus(first, second))


def spread(block):
    turned = block.T
    halves = [
        jnp.concatenate([turned[base + 32 * v : base + 32 * v + 32] for v in range(T)], axis=1)
        for base in (0, 512)
    ]
    return jnp.concatenate(halves, axis=0)


def collect(block):
    parts = [
        block[32 * h : 32 * h + 32, T * v : T * v + T] for h in range(2) for v in range(T)
    ]
    return jnp.concatenate(parts, axis=0).T


def unpacked(axis, small, large):
    tab = {}
    if axis == "y":
        tab["ly"] = small[0:128, 0:192]
        tab["ry"] = (small[128:384, :], small[384:640, :])
    else:
        tab["lxf"], tab["lxi"] = small[0:128, 0:192], small[128:256, 0:192]
        tab["rx"] = (small[256:512, :], small[512:768, :])
    for name, at, lanes in (("t", slice(0, 64), L), ("h", slice(64, 128), L)):
        tab[name + axis] = tuple(large[part, at, 0:lanes] for part in range(2))
    lanes = L if axis == "y" else 128
    tab["b" + axis] = tuple(large[part, 128:136, 0:lanes] for part in range(2))
    return tab


def parts_of(value, at=0):
    return value[:, at : at + L], value[:, at + L : at + 2 * L]


def split3(value):
    high = value.astype(bf16)
    rest = value - high.astype(f32)
    middle = rest.astype(bf16)
    return jnp.concatenate([high, middle, (rest - middle.astype(f32)).astype(bf16)], axis=0)


def lanes_permuted(value, table):
    rows = value.shape[0]
    moved = jnp.dot(split3(value), table, preferred_element_type=f32)
    return moved[:rows] + (moved[rows : 2 * rows] + moved[2 * rows :])


def ramp_of(dy, dx, row_pos):
    lanes = lax.broadcasted_iota(jnp.int32, (8, N), 1)
    which = lax.broadcasted_iota(jnp.int32, (8, N), 0)
    turns = (lanes * dy - 256 * which) & (N - 1)
    wave = jnp.cos(turns.astype(f32) * f32(2.0 * math.pi / N))
    cos_y, sin_y = wave[0:1], wave[1:2]
    kx = lax.broadcasted_iota(jnp.int32, (T, 128), 0) + row_pos * T
    lane = lax.broadcasted_iota(jnp.int32, (T, 128), 1)
    turns = (kx * dx - 256 * lane) & (N - 1)
    wave = jnp.cos(turns.astype(f32) * f32(2.0 * math.pi / N))
    cos_x, sin_x = wave[:, 0:1], wave[:, 1:2]
    return cos_y * cos_x - sin_y * sin_x, cos_y * sin_x + sin_y * cos_x


def first_math(tab, probe, target, ramp):
    spec = tuple(spread(x) for x in mul_conj(probe, ramp))
    spec = rows_join(*y_unfold(spec, tab["by0"]))
    out = times(jnp.concatenate(spec, axis=1), tab["ry0"])
    field = left(tab["ly"], mul((out[:, :L], out[:, L:]), tab["ty"]), -1)
    return jnp.concatenate(field + (lanes_permuted(spread(target), tab["pm"]),), axis=1)


def forward_of(axis):
    return y_forward if axis == "y" else x_forward


def inverse_of(axis):
    return y_inverse if axis == "y" else x_inverse


def propagate(axis, a, tab, conj):
    spec = forward_of(axis)(a, tab)
    times_h = mul_conj if conj else mul
    return inverse_of(axis)(times_h(spec, tab["h" + axis]), tab)


FIRST_LIMIT = 61 * 1024 * 1024
VMEM_LIMIT = 16 * 1024 * 1024


def call(body, axis, operands, out_shapes):
    tables = [jnp.asarray(TAB[axis + bits]) for bits in ("16", "32")] if axis else []
    count = len(operands)

    def kernel(*refs):
        tab = unpacked(axis, *refs[count : count + 2]) if axis else {}
        body(tab, refs[:count], refs[count + len(tables) :])

    return pl.pallas_call(
        kernel,
        out_shape=[jax.ShapeDtypeStruct(shape, f32) for shape in out_shapes],
        in_specs=[pl.BlockSpec(memory_space=pltpu.VMEM)] * (count + len(tables)),
        out_specs=[pl.BlockSpec(memory_space=pltpu.VMEM)] * len(out_shapes),
        compiler_params=pltpu.CompilerParams(vmem_limit_bytes=VMEM_LIMIT),
    )(*operands, *tables)


def first_call(probe, target, offsets):
    names = ("ly", "pm", "first32", "ry0")

    def kernel(offsets_ref, probe_ref, target_ref, ly, pm, small, ry0, out):
        wave = lax.axis_index("section") % 2
        tab = {"ly": ly[...], "pm": pm[...], "ry0": (ry0[0], ry0[1])}
        tab["ty"] = (small[0, 0:64], small[1, 0:64])
        tab["by0"] = (small[0, 64:72], small[1, 64:72])
        ramp = ramp_of(offsets_ref[wave, 0], offsets_ref[wave, 1], lax.axis_index("row"))
        value = first_math(
            tab,
            (probe_ref[0], probe_ref[1]),
            jnp.where(wave == 0, target_ref[0], target_ref[1]),
            ramp,
        )
        put(out, value)

    arrays = [probe, target] + [jnp.asarray(TAB[name]) for name in names]

    def whole(shape):
        return pl.BlockSpec(shape, lambda i: (0,) * len(shape))

    return pl.pallas_call(
        kernel,
        grid=(1,),
        out_shape=jax.ShapeDtypeStruct((6 * B, 128), f32),
        in_specs=[pl.BlockSpec((2, 2), lambda i: (0, 0), memory_space=pltpu.SMEM)]
        + [whole(a.shape) for a in arrays],
        out_specs=whole((6 * B, 128)),
        compiler_params=pltpu.CompilerParams(vmem_limit_bytes=FIRST_LIMIT),
    )(offsets, *arrays)


def exchange(value):
    return lax.all_to_all(value, "row", split_axis=0, concat_axis=0, tiled=True)


def shards(object_slices, probe_spec, offsets, measured):
    own = object_slices[0]
    raw = [lax.ppermute(own, "section", [(s, (s + k) % 4) for s in range(4)]) for k in (1, 2, 3)]
    sent, *raw = lax.optimization_barrier((first_call(probe_spec, measured, offsets), *raw))
    got1 = exchange(sent.reshape(B, 1, 3 * L)).reshape(6 * B, 128)

    def arrange(tab, ins, outs):
        place = lax.axis_index("section")
        for layer in range(4):
            turn = (place - layer) % 4
            for part in range(2):
                value = ins[0][part]
                for k in (1, 2, 3):
                    value = jnp.where(turn == k, ins[k][part], value)
                outs[layer][:, part * L : part * L + L] = spread(value)

    obj = call(arrange, "", (own, *raw), ((B, 2 * L),) * 4)

    def second(tab, ins, outs):
        value = wide(ins[0])
        psi = x_inverse(parts_of(value), tab)
        outs[0][...] = jnp.concatenate(psi, axis=1)
        a = propagate("x", mul(psi, parts_of(ins[1][...])), tab, False)
        put(outs[1], jnp.concatenate(a + (ins[2][...],), axis=1))
        outs[2][...] = value[:, 2 * L :]

    psi0, sent, target = call(
        second,
        "x",
        (got1, obj[0], obj[1]),
        ((B, 2 * L), (8 * B, 128), (B, L)),
    )

    def third(tab, ins, outs):
        value = wide(ins[0])
        psi = propagate("y", parts_of(value), tab, False)
        outs[0][...] = jnp.concatenate(psi, axis=1)
        a = propagate("y", mul(psi, parts_of(value, 2 * L)), tab, False)
        put(outs[1], jnp.concatenate(a, axis=1))

    got2 = exchange(sent)
    psi1, sent = call(third, "y", (got2,), ((B, 2 * L), (4 * B, 128)))

    def fourth(tab, ins, outs):
        psi = propagate("x", parts_of(wide(ins[0])), tab, False)
        outs[0][...] = jnp.concatenate(psi, axis=1)
        a = propagate("x", mul(psi, parts_of(ins[1][...])), tab, False)
        put(outs[1], jnp.concatenate(a + (ins[2][...],), axis=1))

    psi2, sent = call(
        fourth, "x", (exchange(sent), obj[2], obj[3]), ((B, 2 * L), (8 * B, 128))
    )

    def fifth(tab, ins, outs):
        value = wide(ins[0])
        psi = propagate("y", parts_of(value), tab, False)
        outs[0][...] = jnp.concatenate(psi, axis=1)
        a = y_forward(mul(psi, parts_of(value, 2 * L)), tab)
        put(outs[1], jnp.concatenate(a, axis=1))

    got4 = exchange(sent)
    psi3, sent = call(fifth, "y", (got4,), ((B, 2 * L), (4 * B, 128)))

    def far(tab, ins, outs):
        phi = x_forward(parts_of(wide(ins[0])), tab)
        weight = 0.5 * (phi[0] * phi[0] + phi[1] * phi[1] - ins[1][...])
        a = x_inverse((phi[0] * weight, phi[1] * weight), tab)
        put(outs[0], jnp.concatenate(a, axis=1))

    (sent,) = call(far, "x", (exchange(sent), target), ((4 * B, 128),))

    def back_third(tab, ins, outs):
        adj = y_inverse(parts_of(wide(ins[0])), tab)
        grad = mul_conj(adj, parts_of(ins[1][...]))
        a = propagate("y", mul_conj(adj, parts_of(wide(ins[2]), 2 * L)), tab, True)
        put(outs[0], jnp.concatenate(a, axis=1))
        outs[1][...] = jnp.concatenate(grad, axis=1)

    square = ((4 * B, 128), (B, 2 * L))
    sent, grad3 = call(back_third, "y", (exchange(sent), psi3, got4), square)

    def back_second(tab, ins, outs):
        adj = propagate("x", parts_of(wide(ins[0])), tab, True)
        grad = mul_conj(adj, parts_of(ins[1][...]))
        a = propagate("x", mul_conj(adj, parts_of(ins[2][...])), tab, True)
        put(outs[0], jnp.concatenate(a, axis=1))
        outs[1][...] = jnp.concatenate(grad, axis=1)

    sent, grad2 = call(back_second, "x", (exchange(sent), psi2, obj[2]), square)

    def back_first(tab, ins, outs):
        adj = propagate("y", parts_of(wide(ins[0])), tab, True)
        grad = mul_conj(adj, parts_of(ins[1][...]))
        a = propagate("y", mul_conj(adj, parts_of(wide(ins[2]), 2 * L)), tab, True)
        ride = jnp.where(lax.axis_index("section") < 2, jnp.concatenate(grad, axis=1), ins[3][...])
        put(outs[0], jnp.concatenate(a + (ride,), axis=1))

    (sent,) = call(
        back_first, "y", (exchange(sent), psi1, got2, grad3), ((8 * B, 128),)
    )

    def last(tab, ins, outs):
        value = wide(ins[0])
        adj = propagate("x", parts_of(value), tab, True)
        grad = mul_conj(adj, parts_of(ins[1][...]))
        pos = lax.axis_index("section")
        other = parts_of(ins[2][...])
        upper = parts_of(value, 2 * L)
        for part in range(2):
            lower = jnp.where(pos < 2, grad[part], other[part])
            outs[0][part] = collect(jnp.where(pos % 2 == 0, upper[part], lower))
            outs[1][:, part * L : part * L + L] = jnp.where(pos % 2 == 0, lower, upper[part])

    given, kept = call(last, "x", (exchange(sent), psi0, grad2), ((2, T, N), (B, 2 * L)))
    taken = lax.ppermute(given, "section", [(0, 1), (1, 0), (2, 3), (3, 2)])

    def lay_out(tab, ins, outs):
        for part in range(2):
            outs[0][part] = collect(ins[0][:, part * L : part * L + L])

    (kept,) = call(lay_out, "", (kept,), ((2, T, N),))
    return (kept + taken)[None]


def solution(mesh):
    placed = (P("section", None, "row", None), P(None, "row", None), P(), P(None, "row", None))
    return jax.shard_map(
        shards,
        mesh=mesh,
        in_specs=placed,
        out_specs=P("section", None, "row", None),
        check_vma=False,
    )
```

```python
import math

import jax
import jax.numpy as jnp
import numpy as np
from jax import lax
from jax.experimental import pallas as pl
from jax.experimental.pallas import tpu as pltpu
from jax.sharding import PartitionSpec as P


N = 1024
B = 64
T = 16
L = T * T
fresnel_coef = 0.37
f32 = jnp.float32
bf16 = jnp.bfloat16


def split2(value):
    high = value.astype(bf16)
    return high, (value - high.astype(f32)).astype(bf16)


def np_split2(table):
    table = np.asarray(table, np.float64).astype(np.float32)
    high = table.astype(bf16)
    low = (table - high.astype(np.float32)).astype(bf16)
    return high, low


def left_table(cosine, sine):
    both = np.concatenate([cosine, sine], axis=0)
    high, low = np_split2(both)
    return np.concatenate([high, low, high], axis=1)


def pair(angle, scale=1.0):
    return np.stack([np.cos(angle), np.sin(angle)]).astype(np.float32) * np.float32(scale)


def complex_matrix(angle, scale):
    cosine, sine = np.cos(angle) * scale, np.sin(angle) * scale
    return np.concatenate(
        [np.concatenate([cosine, -sine], axis=1), np.concatenate([sine, cosine], axis=1)], axis=0
    )


def make_tables():
    two_pi = 2.0 * math.pi
    r32 = np.arange(32)
    r16 = np.arange(16)
    r8 = np.arange(8)
    blocks = np.arange(B)
    hb, ab = blocks // 32, blocks % 32
    lane_v, lane_t = np.repeat(r16, 16), np.tile(r16, 16)
    tab = {}
    angle = two_pi * np.outer(r32, r32) / 32
    eye2 = np.eye(2)
    tab["ly"] = left_table(np.kron(eye2, np.cos(angle)) / 8, np.kron(eye2, np.sin(angle)) / 8)
    tab["ty"] = pair(two_pi * (2 * lane_t[None, :] + hb[:, None]) * ab[:, None] / N)
    small = two_pi * np.outer(r16, r16) / 16
    mat = complex_matrix(small, 0.25)
    mat = mat.reshape(2, 16, 2, 16)
    full = np.einsum("atbk,vw->avtbwk", mat, np.eye(8)).reshape(256, 256)
    tab["ry"] = np.stack(np_split2(full))
    half = np.broadcast_to(two_pi * lane_t[None, :] / 32, (8, L))
    tab["by"] = pair(half)
    tab["by0"] = pair(np.broadcast_to(two_pi * lane_v[None, :] / 32, (8, L)))
    q = 2 * ab + hb
    angle = two_pi * np.outer(blocks, q) / B
    tab["lxf"] = left_table(np.cos(angle) / 8, np.sin(angle) / 8)
    tab["lxi"] = left_table(np.cos(angle.T) / 8, np.sin(angle.T) / 8)
    place = lane_v // 8 + 2 * (lane_v % 8)
    tab["tx"] = pair(two_pi * q[:, None] * place[None, :] / N)
    mat = complex_matrix(two_pi * np.outer(r8, r8) / 8, 0.25).reshape(2, 8, 2, 8)
    full = np.einsum("avbw,ts->avtbws", mat, np.eye(16)).reshape(256, 256)
    tab["rx"] = np.stack(np_split2(full))
    tab["bx"] = pair(np.broadcast_to(two_pi * np.repeat(r8, 16)[None, :] / 16, (8, 128)))
    signed = lambda freq: np.where(freq < N // 2, freq, freq - N).astype(np.float64)
    ky = ab[:, None] + 32 * lane_t[None, :] + 512 * hb[:, None]
    kx = 16 * blocks[:, None] + place[None, :]
    tab["hy"] = pair(-math.pi * fresnel_coef / N * signed(ky) ** 2)
    tab["hx"] = pair(-math.pi * fresnel_coef / N * signed(kx) ** 2)
    mat = complex_matrix(-small, 0.25).reshape(2, 16, 2, 16)
    order = np.zeros((16, 16))
    spot = np.arange(16)
    order[spot // 8 + 2 * (spot % 8), spot] = 1.0
    full = np.einsum("akbt,uw->akubwt", mat, order).reshape(512, 512)
    tab["ry0"] = np.stack(np_split2(full))
    tab["pm"] = np.einsum("kl,uw->kuwl", np.eye(16), order).reshape(256, 256).astype(bf16)
    return tab


def packed(tab):
    wide = lambda table: np.pad(np.asarray(table), ((0, 0), (0, L - table.shape[1])))
    rows = lambda parts: np.concatenate([wide(part) for part in parts], axis=0)
    both = lambda names: np.stack([rows([tab[n][part] for n in names]) for part in range(2)])
    return {
        "y16": rows([tab["ly"], tab["ry"][0], tab["ry"][1]]),
        "y32": both(("ty", "hy", "by")),
        "x16": rows([tab["lxf"], tab["lxi"], tab["rx"][0], tab["rx"][1]]),
        "x32": both(("tx", "hx", "bx")),
        "first32": both(("ty", "by0")),
        "ry0": tab["ry0"],
        "ly": tab["ly"],
        "pm": tab["pm"],
    }


TAB = packed(make_tables())


def wide(ref):
    count = ref.shape[0] // B
    return jnp.concatenate(
        [ref[pl.ds(i, B, stride=count), :] for i in range(count)], axis=1
    )


def put(ref, value):
    count = ref.shape[0] // B
    for i in range(count):
        ref[pl.ds(i, B, stride=count), :] = value[:, 128 * i : 128 * i + 128]


def mul(a, t):
    return a[0] * t[0] - a[1] * t[1], a[0] * t[1] + a[1] * t[0]


def mul_conj(a, t):
    return a[0] * t[0] + a[1] * t[1], a[1] * t[0] - a[0] * t[1]


def left(table, a, sign):
    high, low = split2(jnp.concatenate(a, axis=1))
    stacked = jnp.concatenate([high, high, low], axis=0)
    out = jnp.dot(table, stacked, preferred_element_type=f32)
    c_re, c_im, s_re, s_im = out[:B, :L], out[:B, L:], out[B:, :L], out[B:, L:]
    if sign > 0:
        return c_re + s_im, c_im - s_re
    return c_re - s_im, c_im + s_re


def times(data, table):
    rows = data.shape[0]
    high, low = split2(data)
    out = jnp.dot(jnp.concatenate([high, low], axis=0), table[0], preferred_element_type=f32)
    return out[:rows] + out[rows:] + jnp.dot(high, table[1], preferred_element_type=f32)


def right(table, a, sign):
    re, im = a
    if sign < 0:
        im = -im
    stacked = jnp.concatenate(
        [
            jnp.concatenate([re[:, :128], im[:, :128]], axis=1),
            jnp.concatenate([re[:, 128:], im[:, 128:]], axis=1),
        ],
        axis=0,
    )
    out = times(stacked, table)
    re = jnp.concatenate([out[:B, :128], out[B:, :128]], axis=1)
    im = jnp.concatenate([out[:B, 128:], out[B:, 128:]], axis=1)
    return (re, im) if sign > 0 else (re, -im)


def rows_join(a, b):
    return tuple(jnp.concatenate([x, y], axis=0) for x, y in zip(a, b))


def lanes_join(a, b):
    return tuple(jnp.concatenate([x, y], axis=1) for x, y in zip(a, b))


def plus(a, b):
    return a[0] + b[0], a[1] + b[1]


def minus(a, b):
    return a[0] - b[0], a[1] - b[1]


def y_forward(a, tab):
    a = left(tab["ly"], a, 1)
    a = mul_conj(a, tab["ty"])
    a = right(tab["ry"], a, 1)
    first = tuple(x[:32] for x in a)
    second = mul_conj(tuple(x[32:] for x in a), tuple(x[:1] for x in tab["by"]))
    return rows_join(plus(first, second), minus(first, second))


def y_unfold(a, turn):
    first, second = tuple(x[:32] for x in a), tuple(x[32:] for x in a)
    return plus(first, second), mul(minus(first, second), tuple(x[:1] for x in turn))


def y_inverse(a, tab):
    a = right(tab["ry"], rows_join(*y_unfold(a, tab["by"])), -1)
    a = mul(a, tab["ty"])
    return left(tab["ly"], a, -1)


def x_forward(a, tab):
    first, second = tuple(x[:, :128] for x in a), tuple(x[:, 128:] for x in a)
    turned = mul_conj(minus(first, second), tuple(x[:1] for x in tab["bx"]))
    a = right(tab["rx"], lanes_join(plus(first, second), turned), 1)
    a = mul_conj(a, tab["tx"])
    return left(tab["lxf"], a, 1)


def x_inverse(a, tab):
    a = left(tab["lxi"], a, -1)
    a = mul(a, tab["tx"])
    a = right(tab["rx"], a, -1)
    first = tuple(x[:, :128] for x in a)
    second = mul(tuple(x[:, 128:] for x in a), tuple(x[:1] for x in tab["bx"]))
    return lanes_join(plus(first, second), minus(first, second))


def spread(block):
    turned = block.T
    halves = [
        jnp.concatenate([turned[base + 32 * v : base + 32 * v + 32] for v in range(T)], axis=1)
        for base in (0, 512)
    ]
    return jnp.concatenate(halves, axis=0)


def collect(block):
    parts = [
        block[32 * h : 32 * h + 32, T * v : T * v + T] for h in range(2) for v in range(T)
    ]
    return jnp.concatenate(parts, axis=0).T


def unpacked(axis, small, large):
    tab = {}
    if axis == "y":
        tab["ly"] = small[0:128, 0:192]
        tab["ry"] = (small[128:384, :], small[384:640, :])
    else:
        tab["lxf"], tab["lxi"] = small[0:128, 0:192], small[128:256, 0:192]
        tab["rx"] = (small[256:512, :], small[512:768, :])
    for name, at, lanes in (("t", slice(0, 64), L), ("h", slice(64, 128), L)):
        tab[name + axis] = tuple(large[part, at, 0:lanes] for part in range(2))
    lanes = L if axis == "y" else 128
    tab["b" + axis] = tuple(large[part, 128:136, 0:lanes] for part in range(2))
    return tab


def parts_of(value, at=0):
    return value[:, at : at + L], value[:, at + L : at + 2 * L]


def split3(value):
    high = value.astype(bf16)
    rest = value - high.astype(f32)
    middle = rest.astype(bf16)
    return jnp.concatenate([high, middle, (rest - middle.astype(f32)).astype(bf16)], axis=0)


def lanes_permuted(value, table):
    rows = value.shape[0]
    moved = jnp.dot(split3(value), table, preferred_element_type=f32)
    return moved[:rows] + (moved[rows : 2 * rows] + moved[2 * rows :])


def ramp_of(dy, dx, row_pos):
    lanes = lax.broadcasted_iota(jnp.int32, (8, N), 1)
    which = lax.broadcasted_iota(jnp.int32, (8, N), 0)
    turns = (lanes * dy - 256 * which) & (N - 1)
    wave = jnp.cos(turns.astype(f32) * f32(2.0 * math.pi / N))
    cos_y, sin_y = wave[0:1], wave[1:2]
    kx = lax.broadcasted_iota(jnp.int32, (T, 128), 0) + row_pos * T
    lane = lax.broadcasted_iota(jnp.int32, (T, 128), 1)
    turns = (kx * dx - 256 * lane) & (N - 1)
    wave = jnp.cos(turns.astype(f32) * f32(2.0 * math.pi / N))
    cos_x, sin_x = wave[:, 0:1], wave[:, 1:2]
    return cos_y * cos_x - sin_y * sin_x, cos_y * sin_x + sin_y * cos_x


def first_math(tab, probe, target, ramp):
    spec = tuple(spread(x) for x in mul_conj(probe, ramp))
    spec = rows_join(*y_unfold(spec, tab["by0"]))
    out = times(jnp.concatenate(spec, axis=1), tab["ry0"])
    field = left(tab["ly"], mul((out[:, :L], out[:, L:]), tab["ty"]), -1)
    return jnp.concatenate(field + (lanes_permuted(spread(target), tab["pm"]),), axis=1)


def forward_of(axis):
    return y_forward if axis == "y" else x_forward


def inverse_of(axis):
    return y_inverse if axis == "y" else x_inverse


def propagate(axis, a, tab, conj):
    spec = forward_of(axis)(a, tab)
    times_h = mul_conj if conj else mul
    return inverse_of(axis)(times_h(spec, tab["h" + axis]), tab)


FIRST_LIMIT = 61 * 1024 * 1024
VMEM_LIMIT = 16 * 1024 * 1024


def call(body, axis, operands, out_shapes):
    tables = [jnp.asarray(TAB[axis + bits]) for bits in ("16", "32")] if axis else []
    count = len(operands)

    def kernel(*refs):
        tab = unpacked(axis, *refs[count : count + 2]) if axis else {}
        body(tab, refs[:count], refs[count + len(tables) :])

    return pl.pallas_call(
        kernel,
        out_shape=[jax.ShapeDtypeStruct(shape, f32) for shape in out_shapes],
        in_specs=[pl.BlockSpec(memory_space=pltpu.VMEM)] * (count + len(tables)),
        out_specs=[pl.BlockSpec(memory_space=pltpu.VMEM)] * len(out_shapes),
        compiler_params=pltpu.CompilerParams(vmem_limit_bytes=VMEM_LIMIT),
    )(*operands, *tables)


def first_call(probe, target, offsets):
    names = ("ly", "pm", "first32", "ry0")

    def kernel(offsets_ref, probe_ref, target_ref, ly, pm, small, ry0, out):
        wave = lax.axis_index("section") % 2
        tab = {"ly": ly[...], "pm": pm[...], "ry0": (ry0[0], ry0[1])}
        tab["ty"] = (small[0, 0:64], small[1, 0:64])
        tab["by0"] = (small[0, 64:72], small[1, 64:72])
        ramp = ramp_of(offsets_ref[wave, 0], offsets_ref[wave, 1], lax.axis_index("row"))
        value = first_math(
            tab,
            (probe_ref[0], probe_ref[1]),
            jnp.where(wave == 0, target_ref[0], target_ref[1]),
            ramp,
        )
        put(out, value)

    arrays = [probe, target] + [jnp.asarray(TAB[name]) for name in names]

    def whole(shape):
        return pl.BlockSpec(shape, lambda i: (0,) * len(shape))

    return pl.pallas_call(
        kernel,
        grid=(1,),
        out_shape=jax.ShapeDtypeStruct((6 * B, 128), f32),
        in_specs=[pl.BlockSpec((2, 2), lambda i: (0, 0), memory_space=pltpu.SMEM)]
        + [whole(a.shape) for a in arrays],
        out_specs=whole((6 * B, 128)),
        compiler_params=pltpu.CompilerParams(vmem_limit_bytes=FIRST_LIMIT),
    )(offsets, *arrays)


def exchange(value):
    return lax.all_to_all(value, "row", split_axis=0, concat_axis=0, tiled=True)


def shards(object_slices, probe_spec, offsets, measured):
    own = object_slices[0]
    def moved(k):
        return lax.ppermute(own, "section", [(s, (s + k) % 4) for s in range(4)])

    behind, ahead, across = moved(3), moved(1), moved(2)
    sent, behind, ahead, across = lax.optimization_barrier(
        (first_call(probe_spec, measured, offsets), behind, ahead, across)
    )
    raw = (ahead, across, behind)
    got1 = exchange(sent.reshape(B, 1, 3 * L)).reshape(6 * B, 128)

    def arrange(tab, ins, outs):
        place = lax.axis_index("section")
        for layer in range(4):
            turn = (place - layer) % 4
            for part in range(2):
                value = ins[0][part]
                for k in (1, 2, 3):
                    value = jnp.where(turn == k, ins[k][part], value)
                outs[layer][:, part * L : part * L + L] = spread(value)

    obj = call(arrange, "", (own, *raw), ((B, 2 * L),) * 4)

    def second(tab, ins, outs):
        value = wide(ins[0])
        psi = x_inverse(parts_of(value), tab)
        outs[0][...] = jnp.concatenate(psi, axis=1)
        a = propagate("x", mul(psi, parts_of(ins[1][...])), tab, False)
        put(outs[1], jnp.concatenate(a + (ins[2][...],), axis=1))
        outs[2][...] = value[:, 2 * L :]

    psi0, sent, target = call(
        second,
        "x",
        (got1, obj[0], obj[1]),
        ((B, 2 * L), (8 * B, 128), (B, L)),
    )

    def third(tab, ins, outs):
        value = wide(ins[0])
        psi = propagate("y", parts_of(value), tab, False)
        outs[0][...] = jnp.concatenate(psi, axis=1)
        a = propagate("y", mul(psi, parts_of(value, 2 * L)), tab, False)
        put(outs[1], jnp.concatenate(a, axis=1))

    got2 = exchange(sent)
    psi1, sent = call(third, "y", (got2,), ((B, 2 * L), (4 * B, 128)))

    def fourth(tab, ins, outs):
        psi = propagate("x", parts_of(wide(ins[0])), tab, False)
        outs[0][...] = jnp.concatenate(psi, axis=1)
        a = propagate("x", mul(psi, parts_of(ins[1][...])), tab, False)
        put(outs[1], jnp.concatenate(a + (ins[2][...],), axis=1))

    psi2, sent = call(
        fourth, "x", (exchange(sent), obj[2], obj[3]), ((B, 2 * L), (8 * B, 128))
    )

    def fifth(tab, ins, outs):
        value = wide(ins[0])
        psi = propagate("y", parts_of(value), tab, False)
        outs[0][...] = jnp.concatenate(psi, axis=1)
        a = y_forward(mul(psi, parts_of(value, 2 * L)), tab)
        put(outs[1], jnp.concatenate(a, axis=1))

    got4 = exchange(sent)
    psi3, sent = call(fifth, "y", (got4,), ((B, 2 * L), (4 * B, 128)))

    def far(tab, ins, outs):
        phi = x_forward(parts_of(wide(ins[0])), tab)
        weight = 0.5 * (phi[0] * phi[0] + phi[1] * phi[1] - ins[1][...])
        a = x_inverse((phi[0] * weight, phi[1] * weight), tab)
        put(outs[0], jnp.concatenate(a, axis=1))

    (sent,) = call(far, "x", (exchange(sent), target), ((4 * B, 128),))

    def back_third(tab, ins, outs):
        adj = y_inverse(parts_of(wide(ins[0])), tab)
        grad = mul_conj(adj, parts_of(ins[1][...]))
        a = propagate("y", mul_conj(adj, parts_of(wide(ins[2]), 2 * L)), tab, True)
        put(outs[0], jnp.concatenate(a, axis=1))
        outs[1][...] = jnp.concatenate(grad, axis=1)

    square = ((4 * B, 128), (B, 2 * L))
    sent, grad3 = call(back_third, "y", (exchange(sent), psi3, got4), square)

    def back_second(tab, ins, outs):
        adj = propagate("x", parts_of(wide(ins[0])), tab, True)
        grad = mul_conj(adj, parts_of(ins[1][...]))
        a = propagate("x", mul_conj(adj, parts_of(ins[2][...])), tab, True)
        put(outs[0], jnp.concatenate(a, axis=1))
        outs[1][...] = jnp.concatenate(grad, axis=1)

    sent, grad2 = call(back_second, "x", (exchange(sent), psi2, obj[2]), square)

    def back_first(tab, ins, outs):
        adj = propagate("y", parts_of(wide(ins[0])), tab, True)
        grad = mul_conj(adj, parts_of(ins[1][...]))
        a = propagate("y", mul_conj(adj, parts_of(wide(ins[2]), 2 * L)), tab, True)
        ride = jnp.where(lax.axis_index("section") < 2, jnp.concatenate(grad, axis=1), ins[3][...])
        put(outs[0], jnp.concatenate(a + (ride,), axis=1))

    (sent,) = call(
        back_first, "y", (exchange(sent), psi1, got2, grad3), ((8 * B, 128),)
    )

    def last(tab, ins, outs):
        value = wide(ins[0])
        adj = propagate("x", parts_of(value), tab, True)
        grad = mul_conj(adj, parts_of(ins[1][...]))
        pos = lax.axis_index("section")
        other = parts_of(ins[2][...])
        upper = parts_of(value, 2 * L)
        for part in range(2):
            lower = jnp.where(pos < 2, grad[part], other[part])
            outs[0][part] = collect(jnp.where(pos % 2 == 0, upper[part], lower))
            outs[1][:, part * L : part * L + L] = jnp.where(pos % 2 == 0, lower, upper[part])

    given, kept = call(last, "x", (exchange(sent), psi0, grad2), ((2, T, N), (B, 2 * L)))
    taken = lax.ppermute(given, "section", [(0, 1), (1, 0), (2, 3), (3, 2)])

    def lay_out(tab, ins, outs):
        for part in range(2):
            outs[0][part] = collect(ins[0][:, part * L : part * L + L])

    (kept,) = call(lay_out, "", (kept,), ((2, T, N),))
    return (kept + taken)[None]


def solution(mesh):
    placed = (P("section", None, "row", None), P(None, "row", None), P(), P(None, "row", None))
    return jax.shard_map(
        shards,
        mesh=mesh,
        in_specs=placed,
        out_specs=P("section", None, "row", None),
        check_vma=False,
    )
```

```python
import math

import jax
import jax.numpy as jnp
import numpy as np
from jax import lax
from jax.experimental import pallas as pl
from jax.experimental.pallas import tpu as pltpu
from jax.sharding import PartitionSpec as P


N = 1024
B = 64
T = 16
L = T * T
fresnel_coef = 0.37
f32 = jnp.float32
bf16 = jnp.bfloat16


def split2(value):
    high = value.astype(bf16)
    return high, (value - high.astype(f32)).astype(bf16)


def np_split2(table):
    table = np.asarray(table, np.float64).astype(np.float32)
    high = table.astype(bf16)
    low = (table - high.astype(np.float32)).astype(bf16)
    return high, low


def left_table(cosine, sine):
    both = np.concatenate([cosine, sine], axis=0)
    high, low = np_split2(both)
    return np.concatenate([high, low, high], axis=1)


def pair(angle, scale=1.0):
    return np.stack([np.cos(angle), np.sin(angle)]).astype(np.float32) * np.float32(scale)


def complex_matrix(angle, scale):
    cosine, sine = np.cos(angle) * scale, np.sin(angle) * scale
    return np.concatenate(
        [np.concatenate([cosine, -sine], axis=1), np.concatenate([sine, cosine], axis=1)], axis=0
    )


def make_tables():
    two_pi = 2.0 * math.pi
    r32 = np.arange(32)
    r16 = np.arange(16)
    r8 = np.arange(8)
    blocks = np.arange(B)
    hb, ab = blocks // 32, blocks % 32
    lane_v, lane_t = np.repeat(r16, 16), np.tile(r16, 16)
    tab = {}
    angle = two_pi * np.outer(r32, r32) / 32
    eye2 = np.eye(2)
    tab["ly"] = left_table(np.kron(eye2, np.cos(angle)) / 8, np.kron(eye2, np.sin(angle)) / 8)
    tab["ty"] = pair(two_pi * (2 * lane_t[None, :] + hb[:, None]) * ab[:, None] / N)
    small = two_pi * np.outer(r16, r16) / 16
    mat = complex_matrix(small, 0.25)
    mat = mat.reshape(2, 16, 2, 16)
    full = np.einsum("atbk,vw->avtbwk", mat, np.eye(8)).reshape(256, 256)
    tab["ry"] = np.stack(np_split2(full))
    half = np.broadcast_to(two_pi * lane_t[None, :] / 32, (8, L))
    tab["by"] = pair(half)
    tab["by0"] = pair(np.broadcast_to(two_pi * lane_v[None, :] / 32, (8, L)))
    q = 2 * ab + hb
    angle = two_pi * np.outer(blocks, q) / B
    tab["lxf"] = left_table(np.cos(angle) / 8, np.sin(angle) / 8)
    tab["lxi"] = left_table(np.cos(angle.T) / 8, np.sin(angle.T) / 8)
    place = lane_v // 8 + 2 * (lane_v % 8)
    tab["tx"] = pair(two_pi * q[:, None] * place[None, :] / N)
    mat = complex_matrix(two_pi * np.outer(r8, r8) / 8, 0.25).reshape(2, 8, 2, 8)
    full = np.einsum("avbw,ts->avtbws", mat, np.eye(16)).reshape(256, 256)
    tab["rx"] = np.stack(np_split2(full))
    tab["bx"] = pair(np.broadcast_to(two_pi * np.repeat(r8, 16)[None, :] / 16, (8, 128)))
    signed = lambda freq: np.where(freq < N // 2, freq, freq - N).astype(np.float64)
    ky = ab[:, None] + 32 * lane_t[None, :] + 512 * hb[:, None]
    kx = 16 * blocks[:, None] + place[None, :]
    tab["hy"] = pair(-math.pi * fresnel_coef / N * signed(ky) ** 2)
    tab["hx"] = pair(-math.pi * fresnel_coef / N * signed(kx) ** 2)
    mat = complex_matrix(-small, 0.25).reshape(2, 16, 2, 16)
    order = np.zeros((16, 16))
    spot = np.arange(16)
    order[spot // 8 + 2 * (spot % 8), spot] = 1.0
    full = np.einsum("akbt,uw->akubwt", mat, order).reshape(512, 512)
    tab["ry0"] = np.stack(np_split2(full))
    tab["pm"] = np.einsum("kl,uw->kuwl", np.eye(16), order).reshape(256, 256).astype(bf16)
    return tab


def packed(tab):
    wide = lambda table: np.pad(np.asarray(table), ((0, 0), (0, L - table.shape[1])))
    rows = lambda parts: np.concatenate([wide(part) for part in parts], axis=0)
    both = lambda names: np.stack([rows([tab[n][part] for n in names]) for part in range(2)])
    return {
        "y16": rows([tab["ly"], tab["ry"][0], tab["ry"][1]]),
        "y32": both(("ty", "hy", "by")),
        "x16": rows([tab["lxf"], tab["lxi"], tab["rx"][0], tab["rx"][1]]),
        "x32": both(("tx", "hx", "bx")),
        "first32": both(("ty", "by0")),
        "ry0": tab["ry0"],
        "ly": tab["ly"],
        "pm": tab["pm"],
    }


TAB = packed(make_tables())


def wide(ref):
    count = ref.shape[0] // B
    return jnp.concatenate(
        [ref[pl.ds(i, B, stride=count), :] for i in range(count)], axis=1
    )


def put(ref, value):
    count = ref.shape[0] // B
    for i in range(count):
        ref[pl.ds(i, B, stride=count), :] = value[:, 128 * i : 128 * i + 128]


def mul(a, t):
    return a[0] * t[0] - a[1] * t[1], a[0] * t[1] + a[1] * t[0]


def mul_conj(a, t):
    return a[0] * t[0] + a[1] * t[1], a[1] * t[0] - a[0] * t[1]


def left(table, a, sign):
    high, low = split2(jnp.concatenate(a, axis=1))
    stacked = jnp.concatenate([high, high, low], axis=0)
    out = jnp.dot(table, stacked, preferred_element_type=f32)
    c_re, c_im, s_re, s_im = out[:B, :L], out[:B, L:], out[B:, :L], out[B:, L:]
    if sign > 0:
        return c_re + s_im, c_im - s_re
    return c_re - s_im, c_im + s_re


def times(data, table):
    rows = data.shape[0]
    high, low = split2(data)
    out = jnp.dot(jnp.concatenate([high, low], axis=0), table[0], preferred_element_type=f32)
    return out[:rows] + out[rows:] + jnp.dot(high, table[1], preferred_element_type=f32)


def right(table, a, sign):
    re, im = a
    if sign < 0:
        im = -im
    stacked = jnp.concatenate(
        [
            jnp.concatenate([re[:, :128], im[:, :128]], axis=1),
            jnp.concatenate([re[:, 128:], im[:, 128:]], axis=1),
        ],
        axis=0,
    )
    out = times(stacked, table)
    re = jnp.concatenate([out[:B, :128], out[B:, :128]], axis=1)
    im = jnp.concatenate([out[:B, 128:], out[B:, 128:]], axis=1)
    return (re, im) if sign > 0 else (re, -im)


def rows_join(a, b):
    return tuple(jnp.concatenate([x, y], axis=0) for x, y in zip(a, b))


def lanes_join(a, b):
    return tuple(jnp.concatenate([x, y], axis=1) for x, y in zip(a, b))


def plus(a, b):
    return a[0] + b[0], a[1] + b[1]


def minus(a, b):
    return a[0] - b[0], a[1] - b[1]


def y_forward(a, tab):
    a = left(tab["ly"], a, 1)
    a = mul_conj(a, tab["ty"])
    a = right(tab["ry"], a, 1)
    first = tuple(x[:32] for x in a)
    second = mul_conj(tuple(x[32:] for x in a), tuple(x[:1] for x in tab["by"]))
    return rows_join(plus(first, second), minus(first, second))


def y_unfold(a, turn):
    first, second = tuple(x[:32] for x in a), tuple(x[32:] for x in a)
    return plus(first, second), mul(minus(first, second), tuple(x[:1] for x in turn))


def y_inverse(a, tab):
    a = right(tab["ry"], rows_join(*y_unfold(a, tab["by"])), -1)
    a = mul(a, tab["ty"])
    return left(tab["ly"], a, -1)


def x_forward(a, tab):
    first, second = tuple(x[:, :128] for x in a), tuple(x[:, 128:] for x in a)
    turned = mul_conj(minus(first, second), tuple(x[:1] for x in tab["bx"]))
    a = right(tab["rx"], lanes_join(plus(first, second), turned), 1)
    a = mul_conj(a, tab["tx"])
    return left(tab["lxf"], a, 1)


def x_inverse(a, tab):
    a = left(tab["lxi"], a, -1)
    a = mul(a, tab["tx"])
    a = right(tab["rx"], a, -1)
    first = tuple(x[:, :128] for x in a)
    second = mul(tuple(x[:, 128:] for x in a), tuple(x[:1] for x in tab["bx"]))
    return lanes_join(plus(first, second), minus(first, second))


def spread(block):
    turned = block.T
    halves = [
        jnp.concatenate([turned[base + 32 * v : base + 32 * v + 32] for v in range(T)], axis=1)
        for base in (0, 512)
    ]
    return jnp.concatenate(halves, axis=0)


def collect(block):
    parts = [
        block[32 * h : 32 * h + 32, T * v : T * v + T] for h in range(2) for v in range(T)
    ]
    return jnp.concatenate(parts, axis=0).T


def unpacked(axis, small, large):
    tab = {}
    if axis == "y":
        tab["ly"] = small[0:128, 0:192]
        tab["ry"] = (small[128:384, :], small[384:640, :])
    else:
        tab["lxf"], tab["lxi"] = small[0:128, 0:192], small[128:256, 0:192]
        tab["rx"] = (small[256:512, :], small[512:768, :])
    for name, at, lanes in (("t", slice(0, 64), L), ("h", slice(64, 128), L)):
        tab[name + axis] = tuple(large[part, at, 0:lanes] for part in range(2))
    lanes = L if axis == "y" else 128
    tab["b" + axis] = tuple(large[part, 128:136, 0:lanes] for part in range(2))
    return tab


def parts_of(value, at=0):
    return value[:, at : at + L], value[:, at + L : at + 2 * L]


def split3(value):
    high = value.astype(bf16)
    rest = value - high.astype(f32)
    middle = rest.astype(bf16)
    return jnp.concatenate([high, middle, (rest - middle.astype(f32)).astype(bf16)], axis=0)


def lanes_permuted(value, table):
    rows = value.shape[0]
    moved = jnp.dot(split3(value), table, preferred_element_type=f32)
    return moved[:rows] + (moved[rows : 2 * rows] + moved[2 * rows :])


def ramp_of(dy, dx, row_pos):
    lanes = lax.broadcasted_iota(jnp.int32, (8, N), 1)
    which = lax.broadcasted_iota(jnp.int32, (8, N), 0)
    turns = (lanes * dy - 256 * which) & (N - 1)
    wave = jnp.cos(turns.astype(f32) * f32(2.0 * math.pi / N))
    cos_y, sin_y = wave[0:1], wave[1:2]
    kx = lax.broadcasted_iota(jnp.int32, (T, 128), 0) + row_pos * T
    lane = lax.broadcasted_iota(jnp.int32, (T, 128), 1)
    turns = (kx * dx - 256 * lane) & (N - 1)
    wave = jnp.cos(turns.astype(f32) * f32(2.0 * math.pi / N))
    cos_x, sin_x = wave[:, 0:1], wave[:, 1:2]
    return cos_y * cos_x - sin_y * sin_x, cos_y * sin_x + sin_y * cos_x


def first_math(tab, probe, target, ramp):
    spec = tuple(spread(x) for x in mul_conj(probe, ramp))
    spec = rows_join(*y_unfold(spec, tab["by0"]))
    out = times(jnp.concatenate(spec, axis=1), tab["ry0"])
    field = left(tab["ly"], mul((out[:, :L], out[:, L:]), tab["ty"]), -1)
    return jnp.concatenate(field + (lanes_permuted(spread(target), tab["pm"]),), axis=1)


def forward_of(axis):
    return y_forward if axis == "y" else x_forward


def inverse_of(axis):
    return y_inverse if axis == "y" else x_inverse


def propagate(axis, a, tab, conj):
    spec = forward_of(axis)(a, tab)
    times_h = mul_conj if conj else mul
    return inverse_of(axis)(times_h(spec, tab["h" + axis]), tab)


FIRST_LIMIT = 61 * 1024 * 1024
VMEM_LIMIT = 16 * 1024 * 1024


def call(body, axis, operands, out_shapes):
    tables = [jnp.asarray(TAB[axis + bits]) for bits in ("16", "32")] if axis else []
    count = len(operands)

    def kernel(*refs):
        tab = unpacked(axis, *refs[count : count + 2]) if axis else {}
        body(tab, refs[:count], refs[count + len(tables) :])

    return pl.pallas_call(
        kernel,
        out_shape=[jax.ShapeDtypeStruct(shape, f32) for shape in out_shapes],
        in_specs=[pl.BlockSpec(memory_space=pltpu.VMEM)] * (count + len(tables)),
        out_specs=[pl.BlockSpec(memory_space=pltpu.VMEM)] * len(out_shapes),
        compiler_params=pltpu.CompilerParams(vmem_limit_bytes=VMEM_LIMIT),
    )(*operands, *tables)


def first_call(probe, target, offsets):
    names = ("ly", "pm", "first32", "ry0")

    def kernel(offsets_ref, probe_ref, target_ref, ly, pm, small, ry0, out):
        wave = lax.axis_index("section") % 2
        tab = {"ly": ly[...], "pm": pm[...], "ry0": (ry0[0], ry0[1])}
        tab["ty"] = (small[0, 0:64], small[1, 0:64])
        tab["by0"] = (small[0, 64:72], small[1, 64:72])
        ramp = ramp_of(offsets_ref[wave, 0], offsets_ref[wave, 1], lax.axis_index("row"))
        value = first_math(
            tab,
            (probe_ref[0], probe_ref[1]),
            jnp.where(wave == 0, target_ref[0], target_ref[1]),
            ramp,
        )
        put(out, value)

    arrays = [probe, target] + [jnp.asarray(TAB[name]) for name in names]

    def whole(shape):
        return pl.BlockSpec(shape, lambda i: (0,) * len(shape))

    return pl.pallas_call(
        kernel,
        grid=(1,),
        out_shape=jax.ShapeDtypeStruct((6 * B, 128), f32),
        in_specs=[pl.BlockSpec((2, 2), lambda i: (0, 0), memory_space=pltpu.SMEM)]
        + [whole(a.shape) for a in arrays],
        out_specs=whole((6 * B, 128)),
        compiler_params=pltpu.CompilerParams(vmem_limit_bytes=FIRST_LIMIT),
    )(offsets, *arrays)


def exchange(value):
    return lax.all_to_all(value, "row", split_axis=0, concat_axis=0, tiled=True)


def shards(object_slices, probe_spec, offsets, measured):
    own = object_slices[0]
    def moved(k):
        return lax.ppermute(own, "section", [(s, (s + k) % 4) for s in range(4)])

    behind, ahead, across = moved(3), moved(1), moved(2)
    sent, behind, ahead, across = lax.optimization_barrier(
        (first_call(probe_spec, measured, offsets), behind, ahead, across)
    )
    raw = (ahead, across, behind)
    got1 = exchange(sent.reshape(B, 1, 3 * L)).reshape(6 * B, 128)

    def arrange(tab, ins, outs):
        place = lax.axis_index("section")
        for layer in range(4):
            turn = (place - layer) % 4
            for part in range(2):
                value = ins[0][part]
                for k in (1, 2, 3):
                    value = jnp.where(turn == k, ins[k][part], value)
                outs[layer][:, part * L : part * L + L] = spread(value)

    obj = call(arrange, "", (own, *raw), ((B, 2 * L),) * 4)

    def second(tab, ins, outs):
        value = wide(ins[0])
        psi = x_inverse(parts_of(value), tab)
        outs[0][...] = jnp.concatenate(psi, axis=1)
        a = propagate("x", mul(psi, parts_of(ins[1][...])), tab, False)
        put(outs[1], jnp.concatenate(a + (ins[2][...],), axis=1))
        outs[2][...] = value[:, 2 * L :]

    psi0, sent, target = call(
        second,
        "x",
        (got1, obj[0], obj[1]),
        ((B, 2 * L), (8 * B, 128), (B, L)),
    )

    def third(tab, ins, outs):
        value = wide(ins[0])
        psi = propagate("y", parts_of(value), tab, False)
        outs[0][...] = jnp.concatenate(psi, axis=1)
        a = propagate("y", mul(psi, parts_of(value, 2 * L)), tab, False)
        put(outs[1], jnp.concatenate(a + (ins[1][...],), axis=1))

    got2 = exchange(sent)
    psi1, sent = call(third, "y", (got2, obj[3]), ((B, 2 * L), (8 * B, 128)))

    def fourth(tab, ins, outs):
        psi = propagate("x", parts_of(wide(ins[0])), tab, False)
        outs[0][...] = jnp.concatenate(psi, axis=1)
        a = propagate("x", mul(psi, parts_of(ins[1][...])), tab, False)
        put(outs[1], jnp.concatenate(a, axis=1))

    got3 = exchange(sent)
    psi2, sent = call(
        fourth, "x", (got3, obj[2]), ((B, 2 * L), (4 * B, 128))
    )

    def fifth(tab, ins, outs):
        value = wide(ins[0])
        psi = propagate("y", parts_of(value), tab, False)
        outs[0][...] = jnp.concatenate(psi, axis=1)
        a = y_forward(mul(psi, parts_of(wide(ins[1]), 2 * L)), tab)
        put(outs[1], jnp.concatenate(a, axis=1))

    psi3, sent = call(fifth, "y", (exchange(sent), got3), ((B, 2 * L), (4 * B, 128)))

    def far(tab, ins, outs):
        phi = x_forward(parts_of(wide(ins[0])), tab)
        weight = 0.5 * (phi[0] * phi[0] + phi[1] * phi[1] - ins[1][...])
        a = x_inverse((phi[0] * weight, phi[1] * weight), tab)
        put(outs[0], jnp.concatenate(a, axis=1))

    (sent,) = call(far, "x", (exchange(sent), target), ((4 * B, 128),))

    def back_third(tab, ins, outs):
        adj = y_inverse(parts_of(wide(ins[0])), tab)
        grad = mul_conj(adj, parts_of(ins[1][...]))
        a = propagate("y", mul_conj(adj, parts_of(wide(ins[2]), 2 * L)), tab, True)
        put(outs[0], jnp.concatenate(a, axis=1))
        outs[1][...] = jnp.concatenate(grad, axis=1)

    square = ((4 * B, 128), (B, 2 * L))
    sent, grad3 = call(back_third, "y", (exchange(sent), psi3, got3), square)

    def back_second(tab, ins, outs):
        adj = propagate("x", parts_of(wide(ins[0])), tab, True)
        grad = mul_conj(adj, parts_of(ins[1][...]))
        a = propagate("x", mul_conj(adj, parts_of(ins[2][...])), tab, True)
        put(outs[0], jnp.concatenate(a, axis=1))
        outs[1][...] = jnp.concatenate(grad, axis=1)

    sent, grad2 = call(back_second, "x", (exchange(sent), psi2, obj[2]), square)

    def back_first(tab, ins, outs):
        adj = propagate("y", parts_of(wide(ins[0])), tab, True)
        grad = mul_conj(adj, parts_of(ins[1][...]))
        a = propagate("y", mul_conj(adj, parts_of(wide(ins[2]), 2 * L)), tab, True)
        ride = jnp.where(lax.axis_index("section") < 2, jnp.concatenate(grad, axis=1), ins[3][...])
        put(outs[0], jnp.concatenate(a + (ride,), axis=1))

    (sent,) = call(
        back_first, "y", (exchange(sent), psi1, got2, grad3), ((8 * B, 128),)
    )

    def last(tab, ins, outs):
        value = wide(ins[0])
        adj = propagate("x", parts_of(value), tab, True)
        grad = mul_conj(adj, parts_of(ins[1][...]))
        pos = lax.axis_index("section")
        other = parts_of(ins[2][...])
        upper = parts_of(value, 2 * L)
        for part in range(2):
            lower = jnp.where(pos < 2, grad[part], other[part])
            outs[0][part] = collect(jnp.where(pos % 2 == 0, upper[part], lower))
            outs[1][:, part * L : part * L + L] = jnp.where(pos % 2 == 0, lower, upper[part])

    given, kept = call(last, "x", (exchange(sent), psi0, grad2), ((2, T, N), (B, 2 * L)))
    taken = lax.ppermute(given, "section", [(0, 1), (1, 0), (2, 3), (3, 2)])

    def lay_out(tab, ins, outs):
        for part in range(2):
            outs[0][part] = collect(ins[0][:, part * L : part * L + L])

    (kept,) = call(lay_out, "", (kept,), ((2, T, N),))
    return (kept + taken)[None]


def solution(mesh):
    placed = (P("section", None, "row", None), P(None, "row", None), P(), P(None, "row", None))
    return jax.shard_map(
        shards,
        mesh=mesh,
        in_specs=placed,
        out_specs=P("section", None, "row", None),
        check_vma=False,
    )
```
